128 devices in a mesh: dp: 4 (over y), table: 32 (over z, x, core).
Axes of the slice: x: 4, y: 4, z: 4, core: 2. Of those that a mesh axis runs over, the one named last changes fastest.
Arguments:
- pooled_a: bfloat16 [16384, 32, 32], P('dp', 'table'), may hold values from -6 to 6
- pooled_b: bfloat16 [16384, 32, 64], P('dp', 'table'), may hold values from -6 to 6
- pooled_c: bfloat16 [16384, 32, 128], P('dp', 'table'), may hold values from -6 to 6
- pooled_d: bfloat16 [16384, 32, 256], P('dp', 'table'), may hold values from -6 to 6
- proj_a: bfloat16 [32, 32, 512], P('table'), may hold values from -1 to 1
- proj_b: bfloat16 [32, 64, 512], P('table'), may hold values from -0.75 to 0.75
- proj_c: bfloat16 [32, 128, 512], P('table'), may hold values from -0.5 to 0.5
- proj_d: bfloat16 [32, 256, 512], P('table'), may hold values from -0.375 to 0.375
- slot_table: int32 [128], replicated, may hold values from 0 to 127, each once
- norm_gain: float32 [512], replicated, may hold values from 0.1 to 1.9
- grad_gram: bfloat16 [16384, 128, 128], P(('dp', 'table')), may hold values from -6 to 6
Outputs:
- grad_pooled_a: bfloat16 [16384, 32, 32], P('dp', 'table')
- grad_pooled_b: bfloat16 [16384, 32, 64], P('dp', 'table')
- grad_pooled_c: bfloat16 [16384, 32, 128], P('dp', 'table')
- grad_pooled_d: bfloat16 [16384, 32, 256], P('dp', 'table')
- grad_proj_a: float32 [32, 32, 512], P('table', None, 'dp')
- grad_proj_b: float32 [32, 64, 512], P('table', None, 'dp')
- grad_proj_c: float32 [32, 128, 512], P('table', None, 'dp')
- grad_proj_d: float32 [32, 256, 512], P('table', None, 'dp')
The draws below stay inside these ranges and needn't reach their ends.
Inputs may be any that keep to these rules, and one draw needn't show every extreme that they name: `slot_table`: each table id stands in exactly one slot.
All inputs are finite; a program needn't handle non-finite values.
Results may differ from the reference program's by a relative error of at most 0.014.
Values may be sent and summed in bfloat16 or wider, within the bound.
No kernel may reach another device: no remote copies, remote signals or barrier semaphores. Data moves between devices by JAX's collectives and lax.ppermute only.
A program may use at most 320 MiB of HBM per device.

```python
import math
import jax
import jax.numpy as jnp
from jax import lax

D = 512
WA = 32
WB = 64
WC = 128
WD = 256
NTAB = 128
BATCH = 16384
N_TABLE = 32


def block_scale(own_key, extent, pieces, smallest, top_value):
    gain = 1.0
    for dim, blocks in pieces:
        steps = jax.random.uniform(jax.random.fold_in(jax.random.fold_in(own_key, 6), dim), (blocks,), jnp.float32, smallest / len(pieces), top_value / len(pieces))
        gain = gain * jnp.repeat(jnp.exp(steps), extent[dim] // blocks).reshape((-1,) + (1,) * (len(extent) - 1 - dim))
    return gain


def bell_draw(rng, extent, spread, most, shards=(), kind=jnp.bfloat16):
    values = jax.random.normal(rng, extent, jnp.float32) * spread
    if len(shards) > 0:
        values = block_scale(rng, extent, shards, -0.22, 0.18) * values
    return jnp.clip(values, min=-most, max=most).astype(kind)


def setup_inputs(seed: int = 0) -> dict:
    splits = jax.random.split(jax.random.key(seed), 12)
    pooled_a = bell_draw(splits[0], (BATCH, N_TABLE, WA), 1.0, 6.0, ((0, 4), (1, 32)))
    pooled_b = bell_draw(splits[1], (BATCH, N_TABLE, WB), 1.0, 6.0, ((0, 4), (1, 32)))
    pooled_c = bell_draw(splits[2], (BATCH, N_TABLE, WC), 1.0, 6.0, ((0, 4), (1, 32)))
    pooled_d = bell_draw(splits[3], (BATCH, N_TABLE, WD), 1.0, 6.0, ((0, 4), (1, 32)))
    proj_a = bell_draw(splits[4], (N_TABLE, WA, D), WA ** -0.5, 1.0, ((0, 32),))
    proj_b = bell_draw(splits[5], (N_TABLE, WB, D), WB ** -0.5, 0.75, ((0, 32),))
    proj_c = bell_draw(splits[6], (N_TABLE, WC, D), WC ** -0.5, 0.5, ((0, 32),))
    proj_d = bell_draw(splits[7], (N_TABLE, WD, D), WD ** -0.5, 0.375, ((0, 32),))
    slot_table = jax.random.permutation(splits[8], NTAB).astype(jnp.int32)
    norm_gain = jnp.clip(1.0 + 0.18 * jax.random.normal(splits[9], (D,), jnp.float32), 0.1, 1.9)
    grad_gram = bell_draw(splits[10], (BATCH, NTAB, NTAB), 1.0, 6.0, ((0, 128),))
    return dict(pooled_a=pooled_a, pooled_b=pooled_b, pooled_c=pooled_c, pooled_d=pooled_d, proj_a=proj_a, proj_b=proj_b, proj_c=proj_c, proj_d=proj_d, slot_table=slot_table, norm_gain=norm_gain, grad_gram=grad_gram)


def reference(pooled_a, pooled_b, pooled_c, pooled_d, proj_a, proj_b, proj_c, proj_d, slot_table, norm_gain, grad_gram):
    pooled = (pooled_a, pooled_b, pooled_c, pooled_d)
    projs = (proj_a, proj_b, proj_c, proj_d)
    block = math.gcd(BATCH, 128)
    count = BATCH // block
    ntable = N_TABLE
    blocks_x = tuple((x.reshape(count, block, x.shape[1], x.shape[2]) for x in pooled))
    blocks_g = grad_gram.reshape(count, block, NTAB, NTAB)
    projs32 = tuple((w.astype(jnp.float32) for w in projs))

    def step(acc, item):
        xs, dgram = item
        parts = []
        for k in range(4):
            p = jnp.einsum('rtw,twd->rtd', xs[k].astype(jnp.float32), projs32[k])
            parts.append(p.astype(jnp.bfloat16))
        projected = jnp.concatenate(parts, axis=1)
        pf = projected.astype(jnp.float32)
        inv_rms = lax.rsqrt(lax.optimization_barrier(jnp.mean(pf * pf, axis=-1, keepdims=True)) + 1e-06)
        normed = (pf * inv_rms * norm_gain).astype(jnp.bfloat16)
        slot_grad = dgram[:, slot_table][:, :, slot_table]
        sg = slot_grad.astype(jnp.float32)
        nf = normed.astype(jnp.float32)
        grad_normed = (jnp.einsum('rst,rtd->rsd', sg, nf) + jnp.einsum('rts,rtd->rsd', sg, nf)) / jnp.sqrt(jnp.float32(D))
        h = norm_gain * grad_normed
        grad_projected = (inv_rms * h - pf * inv_rms ** 3 * lax.optimization_barrier(jnp.mean(pf * h, axis=-1, keepdims=True))).astype(jnp.bfloat16)
        gpf = grad_projected.astype(jnp.float32)
        outs = []
        new_acc = []
        for k in range(4):
            piece = gpf[:, k * ntable:(k + 1) * ntable]
            outs.append(jnp.einsum('rtd,twd->rtw', piece, projs32[k]).astype(jnp.bfloat16))
            new_acc.append(acc[k] + jnp.einsum('rtw,rtd->twd', xs[k].astype(jnp.float32), piece))
        return (tuple(new_acc), tuple(outs))
    init = tuple((jnp.zeros(w.shape, jnp.float32) for w in projs))
    acc, outs = lax.scan(step, init, (blocks_x, blocks_g))
    scale = 1.0 / jnp.sqrt(jnp.float32(BATCH))
    grads = tuple((o.reshape(BATCH, o.shape[2], o.shape[3]) for o in outs))
    return (grads[0], grads[1], grads[2], grads[3], acc[0] * scale, acc[1] * scale, acc[2] * scale, acc[3] * scale)
```

```python
import jax
import jax.numpy as jnp
import numpy as np
from jax import lax
from jax.experimental import pallas as pl
from jax.experimental.pallas import tpu as pltpu
from jax.sharding import Mesh, PartitionSpec as P

F32 = jnp.float32
BF16 = jnp.bfloat16
PLANE = ("z", "x", "c")
MIB = 1024 * 1024
ROWS = 224
GROUP = 8
UNROLL = 8


def dot(a, b, dims=((1,), (0,))):
    return lax.dot_general(a, b, (dims, ((), ())), preferred_element_type=F32)


def owner_forward_body(at_ref, bt_ref, c_ref, d_ref, wd_ref, u_ref):
    rows, width = c_ref.shape[0], wd_ref.shape[1]
    narrow = jnp.concatenate(
        [bt_ref[...], at_ref[...], jnp.zeros((32, rows), BF16)], axis=0
    )
    u_ref[:, 0:width] = dot(d_ref[...], wd_ref[...]).astype(BF16)
    u_ref[:, width : width + 128] = c_ref[...]
    u_ref[:, width + 128 : width + 256] = narrow.T


def owner_forward(at, bt, c, d, wd, rows=512):
    total, width = c.shape[0], wd.shape[1]
    return pl.pallas_call(
        owner_forward_body,
        grid=(total // rows,),
        in_specs=[
            pl.BlockSpec((at.shape[0], rows), lambda i: (0, i)),
            pl.BlockSpec((bt.shape[0], rows), lambda i: (0, i)),
            pl.BlockSpec((rows, c.shape[1]), lambda i: (i, 0)),
            pl.BlockSpec((rows, d.shape[1]), lambda i: (i, 0)),
            pl.BlockSpec(wd.shape, lambda i: (0, 0)),
        ],
        out_specs=pl.BlockSpec((rows, width + 256), lambda i: (i, 0)),
        out_shape=jax.ShapeDtypeStruct((total, width + 256), BF16),
        compiler_params=pltpu.CompilerParams(vmem_limit_bytes=40 * MIB),
        cost_estimate=pl.CostEstimate(
            flops=2 * total * 256 * width, bytes_accessed=total * 2 * (480 + 768), transcendentals=0
        ),
        name="owner_forward",
    )(at, bt, c, d, wd)


def padded_weights(w):
    zeros = lambda n: jnp.zeros((n, w.shape[1]), w.dtype)
    wc = w[0:128]
    wb = jnp.concatenate([w[128:192], zeros(64)], axis=0)
    wa = jnp.concatenate([zeros(64), w[192:224], zeros(32)], axis=0)
    return wa, wb, wc


def middle_body(
    steps, at_ref, table_ref, gain_ref, pd_ref, x_ref, w00, w01, w02, w03, w10, w11, w12, w13,
    g_ref, gu_ref, v00, v01, v02, v03, v10, v11, v12, v13, scr, nrm, acc,
):
    i = pl.program_id(0)
    nb = x_ref.shape[1]
    ns = nb + 1
    width = gain_ref.shape[1]
    lanes = range(width // 128)
    plane = 128 * ns
    weights = ((w00, w01, w02, w03), (w10, w11, w12, w13))
    weight_grads = ((v00, v01, v02, v03), (v10, v11, v12, v13))
    z, x, core = at_ref[0], at_ref[1], at_ref[2]

    def put(slot, value):
        start = table_ref[slot] * ns
        for q in lanes:
            scr[pl.ds(q * plane + start, nb), :] = value[:, q * 128 : (q + 1) * 128]

    def take(slot):
        start = table_ref[slot] * ns
        pieces = [scr[pl.ds(q * plane + start, nb), :].astype(BF16) for q in lanes]
        return jnp.concatenate(pieces, axis=1)

    def strided(q, r, b):
        return pl.ds(q * plane + r * ns + b, 32, stride=ns)

    def tables(dz):
        zabs = lax.rem(z - dz + 4, 4)
        for dx in range(4):
            for side in range(2):
                t = lax.rem(x - dx + 4, 4) * 2 + lax.rem(core + side, 2)
                w = jnp.concatenate([weights[side][q][dx] for q in lanes], axis=1)
                yield dx, side, t, zabs * GROUP + t, padded_weights(w)

    @pl.when(i < 4)
    def _():
        for dx, side, t, j, (wa, wb, wc) in tables(i):
            xc = x_ref[t, :, 0:128]
            xn = x_ref[t, :, 128:256]
            put(j, dot(xn, wa).astype(BF16).astype(F32))
            put(32 + j, dot(xn, wb).astype(BF16).astype(F32))
            put(64 + j, dot(xc, wc).astype(BF16).astype(F32))
            put(96 + j, pd_ref[t].astype(F32))

    @pl.when((i >= 4) & (i < 4 + steps))
    def _():
        per = g_ref.shape[0]
        gain = gain_ref[...]
        scaled = gain * (1.0 / np.sqrt(width).astype(np.float32))
        base = (i - 4) * per

        def one(s, u):
            b = base + s
            for r in range(0, 128, 32):
                pf = jnp.concatenate([scr[strided(q, r, b), :] for q in lanes], axis=1)
                inv = lax.rsqrt(jnp.sum(pf * pf, axis=1, keepdims=True) * (1.0 / width) + 1e-06)
                nrm[u, r : r + 32, :] = (pf * inv * gain).astype(BF16)
            g = g_ref[s]
            n = nrm[u]
            acc[u] = dot(jnp.concatenate([g, g.T], axis=1), jnp.concatenate([n, n], axis=0))
            for r in range(0, 128, 32):
                pf = jnp.concatenate([scr[strided(q, r, b), :] for q in lanes], axis=1)
                h = acc[u, r : r + 32, :] * scaled
                inv = lax.rsqrt(jnp.sum(pf * pf, axis=1, keepdims=True) * (1.0 / width) + 1e-06)
                m = jnp.sum(pf * h, axis=1, keepdims=True) * (1.0 / width)
                out = inv * h - pf * (inv * inv * inv * m)
                for q in lanes:
                    scr[strided(q, r, b), :] = out[:, q * 128 : (q + 1) * 128]

        def several(v, carry):
            for u in range(UNROLL):
                one(v * UNROLL + u, u)
            return carry

        lax.fori_loop(0, per // UNROLL, several, 0)

    @pl.when(i >= 4 + steps)
    def _():
        last, first = ((1,), (1,)), ((0,), (0,))
        for dx, side, t, j, (wa, wb, wc) in tables(i - 4 - steps):
            xc = x_ref[t, :, 0:128]
            xn = x_ref[t, :, 128:256]
            ga, gb, gc = take(j), take(32 + j), take(64 + j)
            gu_ref[t, :, 0:width] = take(96 + j)
            gu_ref[t, :, width : width + 128] = dot(gc, wc, last).astype(BF16)
            gu_ref[t, :, width + 128 : width + 256] = (
                dot(ga, wa, last) + dot(gb, wb, last)
            ).astype(BF16)
            vc = dot(xc, gc, first).astype(BF16)
            vb = dot(xn, gb, first)[0:64].astype(BF16)
            va = dot(xn, ga, first)[64:96].astype(BF16)
            for q in lanes:
                part = slice(q * 128, (q + 1) * 128)
                weight_grads[side][q][dx, 0:128, :] = vc[:, part]
                weight_grads[side][q][dx, 128:192, :] = vb[:, part]
                weight_grads[side][q][dx, 192:224, :] = va[:, part]


def middle(at, table, gain, u, ws, g, per=16):
    ntab, nb, full = u.shape
    width = gain.shape[1]
    steps = nb // per

    def turn(i):
        return jnp.where(i < 4, i, jnp.where(i < 4 + steps, 3, i - 4 - steps))

    def by_table(i, at):
        return lax.rem(at[0] - turn(i) + 4, 4)

    def forward_only(i, at):
        return lax.rem(at[0] - jnp.minimum(i, 3) + 4, 4)

    def late(i):
        return jnp.maximum(i - 4 - steps, 0)

    def backward_only(i, at):
        return lax.rem(at[0] - late(i) + 4, 4)

    weight_in = pl.BlockSpec((4, ROWS, 128), lambda i, at, tb: (turn(i), 0, 0))
    weight_out = pl.BlockSpec((4, ROWS, 128), lambda i, at, tb: (late(i), 0, 0))
    return pl.pallas_call(
        lambda *refs: middle_body(steps, *refs),
        grid_spec=pltpu.PrefetchScalarGridSpec(
            num_scalar_prefetch=2,
            grid=(8 + steps,),
            in_specs=[
                pl.BlockSpec((1, width), lambda i, at, tb: (0, 0)),
                pl.BlockSpec((GROUP, nb, width), lambda i, at, tb: (forward_only(i, at), 0, 0)),
                pl.BlockSpec(
                    (GROUP, nb, 256), lambda i, at, tb: (by_table(i, at), 0, width // 256)
                ),
            ]
            + [weight_in] * 8
            + [
                pl.BlockSpec(
                    (per, 128, 128), lambda i, at, tb: (jnp.clip(i - 4, 0, steps - 1), 0, 0)
                ),
            ],
            out_specs=[
                pl.BlockSpec((GROUP, nb, full), lambda i, at, tb: (backward_only(i, at), 0, 0)),
            ]
            + [weight_out] * 8,
            scratch_shapes=[
                pltpu.VMEM((width * (nb + 1), 128), F32),
                pltpu.VMEM((UNROLL, 128, width), BF16),
                pltpu.VMEM((UNROLL, 128, width), F32),
            ],
        ),
        out_shape=[jax.ShapeDtypeStruct((ntab, nb, full), BF16)]
        + [jax.ShapeDtypeStruct((16, ROWS, 128), BF16)] * 8,
        compiler_params=pltpu.CompilerParams(vmem_limit_bytes=58 * MIB),
        cost_estimate=pl.CostEstimate(
            flops=15 * 10**9, bytes_accessed=40 * 10**6, transcendentals=0
        ),
        name="middle",
    )(at, table, gain, u, u, *ws, g)


def owner_backward_body(
    gp_ref, gx_ref, d_ref, wd_ref, gat_ref, gbt_ref, gc_ref, gd_ref, gw_ref, acc
):
    i = pl.program_id(0)
    gc_ref[...] = gx_ref[:, 0:128]
    narrow = gx_ref[:, 128:256].T
    gbt_ref[...] = narrow[0:64]
    gat_ref[...] = narrow[64:96]
    gp = gp_ref[...]
    gd_ref[...] = dot(gp, wd_ref[...], ((1,), (1,))).astype(BF16)

    @pl.when(i == 0)
    def _():
        acc[...] = jnp.zeros_like(acc)

    acc[...] += dot(d_ref[...], gp, ((0,), (0,)))

    @pl.when(i == pl.num_programs(0) - 1)
    def _():
        gw_ref[...] = acc[...].astype(BF16)


def owner_backward(gu, d, wd, rows=512):
    total = gu.shape[0]
    wdim, width = wd.shape
    return pl.pallas_call(
        owner_backward_body,
        grid=(total // rows,),
        in_specs=[
            pl.BlockSpec((rows, width), lambda i: (i, 0)),
            pl.BlockSpec((rows, 256), lambda i: (i, width // 256)),
            pl.BlockSpec((rows, wdim), lambda i: (i, 0)),
            pl.BlockSpec(wd.shape, lambda i: (0, 0)),
        ],
        out_specs=[
            pl.BlockSpec((32, rows), lambda i: (0, i)),
            pl.BlockSpec((64, rows), lambda i: (0, i)),
            pl.BlockSpec((rows, 128), lambda i: (i, 0)),
            pl.BlockSpec((rows, wdim), lambda i: (i, 0)),
            pl.BlockSpec((wdim, width), lambda i: (0, 0)),
        ],
        out_shape=[
            jax.ShapeDtypeStruct((32, total), BF16),
            jax.ShapeDtypeStruct((64, total), BF16),
            jax.ShapeDtypeStruct((total, 128), BF16),
            jax.ShapeDtypeStruct((total, wdim), BF16),
            jax.ShapeDtypeStruct((wdim, width), BF16),
        ],
        scratch_shapes=[pltpu.VMEM((wdim, width), F32)],
        compiler_params=pltpu.CompilerParams(vmem_limit_bytes=40 * MIB),
        cost_estimate=pl.CostEstimate(
            flops=4 * total * wdim * width, bytes_accessed=total * 2 * 1500, transcendentals=0
        ),
        name="owner_backward",
    )(gu, gu, d, wd)


def exchange(x):
    return lax.all_to_all(x, PLANE, split_axis=0, concat_axis=0, tiled=True)


def shift(x, axis, k):
    n = lax.axis_size(axis)
    return lax.ppermute(x, axis, [(i, (i + k) % n) for i in range(n)])


def add(*parts):
    total = parts[0].astype(F32)
    for p in parts[1:]:
        total = total + p.astype(F32)
    return total


def turn_features(w, y):
    blocks = w.reshape(w.shape[0], 4, 128)
    order = lax.rem(y - jnp.arange(4) + 4, 4)
    return jnp.take(blocks, order, axis=1).reshape(w.shape)


def gather_plane(w, y):
    part = lax.dynamic_slice_in_dim(w, y * 128, 128, axis=1)
    part = jnp.stack([part, shift(part, "x", 1), shift(part, "x", 2), shift(part, "x", -1)])
    return jnp.concatenate([part, shift(part, "z", 1), shift(part, "z", 2), shift(part, "z", -1)])


def gather_quarters(part):
    below, above = shift(part, "y", 1), shift(part, "y", -1)
    far = jnp.concatenate([shift(below[:8], "y", 1), shift(above[8:], "y", -1)])
    own = (part, below, far, above)
    return own + tuple(shift(p, "c", 1) for p in own)


def scatter_weight_grads(own, other):
    s = [add(o, shift(p, "c", 1)).astype(BF16) for o, p in zip(own, other)]
    from_above, from_below = shift(s[2][:8], "y", -1), shift(s[2][8:], "y", 1)
    down = jnp.concatenate([add(s[1][:8], from_above).astype(BF16), s[1][8:]])
    up = jnp.concatenate([s[3][:8], add(s[3][8:], from_below).astype(BF16)])
    part = add(s[0], shift(down, "y", -1), shift(up, "y", 1)).astype(BF16)
    for axis in ("z", "x"):
        n = part.shape[0] // 4
        part = add(
            part[:n],
            shift(part[n : 2 * n], axis, -1),
            shift(part[2 * n : 3 * n], axis, -2),
            shift(part[3 * n :], axis, -3),
        ).astype(BF16)
    return part[0]


def on_device(
    pooled_a, pooled_b, pooled_c, pooled_d, proj_a, proj_b, proj_c, proj_d,
    slot_table, norm_gain, grad_gram,
):
    total = pooled_a.shape[0]
    nb = grad_gram.shape[0]
    owners = total // nb
    y = lax.axis_index("y")
    at = jnp.stack([lax.axis_index("z"), lax.axis_index("x"), lax.axis_index("c")]).astype(jnp.int32)
    wd = turn_features(proj_d[0], y)
    gain = turn_features(norm_gain[None], y)
    d = pooled_d[:, 0]
    part = gather_plane(jnp.concatenate([proj_c[0], proj_b[0], proj_a[0]], axis=0), y)
    u = owner_forward(
        pooled_a.transpose(1, 2, 0)[0], pooled_b.transpose(1, 2, 0)[0], pooled_c[:, 0], d, wd
    )
    u, part = lax.optimization_barrier((u, part))
    ws = gather_quarters(part)
    u = exchange(u.reshape(owners, nb, -1))
    gu, *gws = middle(at, slot_table, gain, u, ws, grad_gram)
    gu = exchange(gu).reshape(total, -1)
    gat, gbt, gc, gd, gwd = owner_backward(gu, d, wd)
    scale = 1.0 / np.sqrt(total * lax.axis_size("y")).astype(np.float32)
    gw = scatter_weight_grads(gws[:4], gws[4:]).astype(F32) * scale
    q = [gwd[:, r * 128 : (r + 1) * 128] for r in range(4)]
    gwd = add(q[0], shift(q[1], "y", -1), shift(q[2], "y", -2), shift(q[3], "y", -3)) * scale
    return (
        gat.T[:, None],
        gbt.T[:, None],
        gc[:, None],
        gd[:, None],
        gw[192:224][None],
        gw[128:192][None],
        gw[0:128][None],
        gwd[None],
    )


def solution(mesh):
    fine = Mesh(np.array(mesh.devices).reshape(4, 4, 4, 2), ("y", "z", "x", "c"))
    pooled = P("y", PLANE, None)
    weight = P(PLANE, None, None)
    in_specs = (pooled,) * 4 + (weight,) * 4 + (P(), P(), P(("y",) + PLANE, None, None))
    out_specs = (pooled,) * 4 + (P(PLANE, None, "y"),) * 4
    return jax.shard_map(
        on_device, mesh=fine, in_specs=in_specs, out_specs=out_specs, check_vma=False
    )
```

```python
import jax
import jax.numpy as jnp
import numpy as np
from jax import lax
from jax.experimental import pallas as pl
from jax.experimental.pallas import tpu as pltpu
from jax.sharding import Mesh, PartitionSpec as P

F32 = jnp.float32
BF16 = jnp.bfloat16
PLANE = ("z", "x", "c")
MIB = 1024 * 1024
ROWS = 224
GROUP = 8
UNROLL = 8
PARTS = (5, 3)


def dot(a, b, dims=((1,), (0,))):
    return lax.dot_general(a, b, (dims, ((), ())), preferred_element_type=F32)


def owner_forward_body(at_ref, bt_ref, c_ref, d_ref, wd_ref, *u_refs):
    rows, width = c_ref.shape[0], wd_ref.shape[1]
    narrow = jnp.concatenate(
        [bt_ref[...], at_ref[...], jnp.zeros((32, rows), BF16)], axis=0
    )
    group = u_refs[0].shape[0]

    def place(value, start, stop):
        value = value.reshape(group, rows // group, stop - start)
        first = 0
        for u_ref in u_refs:
            part = u_ref.shape[1]
            u_ref[:, :, start:stop] = value[:, first : first + part]
            first += part

    place(dot(d_ref[...], wd_ref[...]).astype(BF16), 0, width)
    place(c_ref[...], width, width + 128)
    place(narrow.T, width + 128, width + 256)


def owner_forward(at, bt, c, d, wd, nb, rows=512):
    total, width = c.shape[0], wd.shape[1]
    parts = [nb * n // sum(PARTS) for n in PARTS]
    return pl.pallas_call(
        owner_forward_body,
        grid=(total // rows,),
        in_specs=[
            pl.BlockSpec((at.shape[0], rows), lambda i: (0, i)),
            pl.BlockSpec((bt.shape[0], rows), lambda i: (0, i)),
            pl.BlockSpec((rows, c.shape[1]), lambda i: (i, 0)),
            pl.BlockSpec((rows, d.shape[1]), lambda i: (i, 0)),
            pl.BlockSpec(wd.shape, lambda i: (0, 0)),
        ],
        out_specs=[pl.BlockSpec((rows // nb, n, width + 256), lambda i: (i, 0, 0)) for n in parts],
        out_shape=[jax.ShapeDtypeStruct((total // nb, n, width + 256), BF16) for n in parts],
        compiler_params=pltpu.CompilerParams(vmem_limit_bytes=40 * MIB),
        cost_estimate=pl.CostEstimate(
            flops=2 * total * 256 * width, bytes_accessed=total * 2 * (480 + 768), transcendentals=0
        ),
        name="owner_forward",
    )(at, bt, c, d, wd)


def padded_weights(w):
    zeros = lambda n: jnp.zeros((n, w.shape[1]), w.dtype)
    wc = w[0:128]
    wb = jnp.concatenate([w[128:192], zeros(64)], axis=0)
    wa = jnp.concatenate([zeros(64), w[192:224], zeros(32)], axis=0)
    return wa, wb, wc


def middle_body(
    steps, later, at_ref, table_ref, gain_ref, pd_ref, x_ref, w00, w01, w02, w03, w10, w11, w12, w13,
    g_ref, *refs,
):
    before = (refs[0:4], refs[4:8])
    gu_ref, v00, v01, v02, v03, v10, v11, v12, v13, scr, nrm, acc = refs[8 if later else 0 :]
    i = pl.program_id(0)
    nb = x_ref.shape[1]
    ns = nb + 1
    width = gain_ref.shape[1]
    lanes = range(width // 128)
    plane = 128 * ns
    weights = ((w00, w01, w02, w03), (w10, w11, w12, w13))
    weight_grads = ((v00, v01, v02, v03), (v10, v11, v12, v13))
    z, x, core = at_ref[0], at_ref[1], at_ref[2]

    def put(slot, value):
        start = table_ref[slot] * ns
        for q in lanes:
            scr[pl.ds(q * plane + start, nb), :] = value[:, q * 128 : (q + 1) * 128]

    def take(slot):
        start = table_ref[slot] * ns
        pieces = [scr[pl.ds(q * plane + start, nb), :].astype(BF16) for q in lanes]
        return jnp.concatenate(pieces, axis=1)

    def strided(q, r, b):
        return pl.ds(q * plane + r * ns + b, 32, stride=ns)

    def tables(dz):
        zabs = lax.rem(z - dz + 4, 4)
        for dx in range(4):
            for side in range(2):
                t = lax.rem(x - dx + 4, 4) * 2 + lax.rem(core + side, 2)
                w = jnp.concatenate([weights[side][q][dx] for q in lanes], axis=1)
                yield dx, side, t, zabs * GROUP + t, padded_weights(w)

    @pl.when(i < 4)
    def _():
        for dx, side, t, j, (wa, wb, wc) in tables(i):
            xc = x_ref[t, :, 0:128]
            xn = x_ref[t, :, 128:256]
            put(j, dot(xn, wa).astype(BF16).astype(F32))
            put(32 + j, dot(xn, wb).astype(BF16).astype(F32))
            put(64 + j, dot(xc, wc).astype(BF16).astype(F32))
            put(96 + j, pd_ref[t].astype(F32))

    @pl.when((i >= 4) & (i < 4 + steps))
    def _():
        per = g_ref.shape[0]
        gain = gain_ref[...]
        scaled = gain * (1.0 / np.sqrt(width).astype(np.float32))
        base = (i - 4) * per

        def one(s, u):
            b = base + s
            for r in range(0, 128, 32):
                pf = jnp.concatenate([scr[strided(q, r, b), :] for q in lanes], axis=1)
                inv = lax.rsqrt(jnp.sum(pf * pf, axis=1, keepdims=True) * (1.0 / width) + 1e-06)
                nrm[u, r : r + 32, :] = (pf * inv * gain).astype(BF16)
            g = g_ref[s]
            n = nrm[u]
            acc[u] = dot(jnp.concatenate([g, g.T], axis=1), jnp.concatenate([n, n], axis=0))
            for r in range(0, 128, 32):
                pf = jnp.concatenate([scr[strided(q, r, b), :] for q in lanes], axis=1)
                h = acc[u, r : r + 32, :] * scaled
                inv = lax.rsqrt(jnp.sum(pf * pf, axis=1, keepdims=True) * (1.0 / width) + 1e-06)
                m = jnp.sum(pf * h, axis=1, keepdims=True) * (1.0 / width)
                out = inv * h - pf * (inv * inv * inv * m)
                for q in lanes:
                    scr[strided(q, r, b), :] = out[:, q * 128 : (q + 1) * 128]

        def several(v, carry):
            for u in range(UNROLL):
                one(v * UNROLL + u, u)
            return carry

        lax.fori_loop(0, per // UNROLL, several, 0)

    @pl.when(i >= 4 + steps)
    def _():
        last, first = ((1,), (1,)), ((0,), (0,))
        for dx, side, t, j, (wa, wb, wc) in tables(i - 4 - steps):
            xc = x_ref[t, :, 0:128]
            xn = x_ref[t, :, 128:256]
            ga, gb, gc = take(j), take(32 + j), take(64 + j)
            gu_ref[t, :, 0:width] = take(96 + j)
            gu_ref[t, :, width : width + 128] = dot(gc, wc, last).astype(BF16)
            gu_ref[t, :, width + 128 : width + 256] = (
                dot(ga, wa, last) + dot(gb, wb, last)
            ).astype(BF16)
            vc = dot(xc, gc, first)
            vb = dot(xn, gb, first)[0:64]
            va = dot(xn, ga, first)[64:96]
            for q in lanes:
                for value, rows in ((vc, slice(0, 128)), (vb, slice(128, 192)), (va, slice(192, 224))):
                    piece = value[:, q * 128 : (q + 1) * 128]
                    if later:
                        piece = piece + before[side][q][dx, rows, :].astype(F32)
                    weight_grads[side][q][dx, rows, :] = piece.astype(BF16)


def middle(start, at, table, gain, u, ws, g, before, per=16):
    ntab, nb, full = u.shape
    width = gain.shape[1]
    steps = nb // per

    def turn(i):
        return jnp.where(i < 4, i, jnp.where(i < 4 + steps, 3, i - 4 - steps))

    def by_table(i, at):
        return lax.rem(at[0] - turn(i) + 4, 4)

    def forward_only(i, at):
        return lax.rem(at[0] - jnp.minimum(i, 3) + 4, 4)

    def late(i):
        return jnp.maximum(i - 4 - steps, 0)

    def backward_only(i, at):
        return lax.rem(at[0] - late(i) + 4, 4)

    weight_in = pl.BlockSpec((4, ROWS, 128), lambda i, at, tb: (turn(i), 0, 0))
    weight_out = pl.BlockSpec((4, ROWS, 128), lambda i, at, tb: (late(i), 0, 0))
    return pl.pallas_call(
        lambda *refs: middle_body(steps, len(before) > 0, *refs),
        grid_spec=pltpu.PrefetchScalarGridSpec(
            num_scalar_prefetch=2,
            grid=(8 + steps,),
            in_specs=[
                pl.BlockSpec((1, width), lambda i, at, tb: (0, 0)),
                pl.BlockSpec((GROUP, nb, width), lambda i, at, tb: (forward_only(i, at), 0, 0)),
                pl.BlockSpec(
                    (GROUP, nb, 256), lambda i, at, tb: (by_table(i, at), 0, width // 256)
                ),
            ]
            + [weight_in] * 8
            + [
                pl.BlockSpec(
                    (per, 128, 128),
                    lambda i, at, tb: (start // per + jnp.clip(i - 4, 0, steps - 1), 0, 0),
                ),
            ]
            + [weight_out] * len(before),
            out_specs=[
                pl.BlockSpec((GROUP, nb, full), lambda i, at, tb: (backward_only(i, at), 0, 0)),
            ]
            + [weight_out] * 8,
            scratch_shapes=[
                pltpu.VMEM((width * (nb + 1), 128), F32),
                pltpu.VMEM((UNROLL, 128, width), BF16),
                pltpu.VMEM((UNROLL, 128, width), F32),
            ],
        ),
        out_shape=[jax.ShapeDtypeStruct((ntab, nb, full), BF16)]
        + [jax.ShapeDtypeStruct((16, ROWS, 128), BF16)] * 8,
        compiler_params=pltpu.CompilerParams(vmem_limit_bytes=58 * MIB),
        cost_estimate=pl.CostEstimate(
            flops=nb * 10**8, bytes_accessed=35 * 10**6, transcendentals=0
        ),
        name="middle",
    )(at, table, gain, u, u, *ws, g, *before)


def owner_backward_body(later, gp_ref, gx_ref, d_ref, wd_ref, *refs):
    gd_ref, gc_ref, gw_ref, acc = refs[-4:]
    i = pl.program_id(0)
    owners, part, wdim = d_ref.shape
    gp = gp_ref[...].reshape(owners * part, -1)
    gd = dot(gp, wd_ref[...], ((1,), (1,))).astype(BF16)
    gd_ref[...] = gd.reshape(owners, part, wdim)
    gc_ref[...] = gx_ref[...]

    @pl.when(i == 0)
    def _():
        acc[...] = refs[2][...] if later else jnp.zeros_like(acc)

    acc[...] += dot(d_ref[...].reshape(owners * part, wdim), gp, ((0,), (0,)))

    @pl.when(i == pl.num_programs(0) - 1)
    def _():
        gw_ref[...] = acc[...].astype(gw_ref.dtype)


def owner_backward(start, gu, d, wd, before=(), per=16):
    owners, nb, wdim = d.shape
    width = wd.shape[1]
    part = gu.shape[1]
    later = len(before) > 0
    whole = pl.BlockSpec((wdim, width), lambda i: (0, 0))
    d_spec = pl.BlockSpec((owners, per, wdim), lambda i: (0, start // per + i, 0))
    c_spec = pl.BlockSpec((owners, per, 128), lambda i: (0, start // per + i, 0))
    in_specs = [
        pl.BlockSpec((owners, per, width), lambda i: (0, i, 0)),
        pl.BlockSpec((owners, per, 128), lambda i: (0, i, width // 128)),
        d_spec,
        whole,
    ]
    if later:
        in_specs += [pl.BlockSpec(memory_space=pl.ANY)] * 2 + [whole]
    return pl.pallas_call(
        lambda *refs: owner_backward_body(later, *refs),
        grid=(part // per,),
        in_specs=in_specs,
        out_specs=[d_spec, c_spec, whole],
        out_shape=[
            jax.ShapeDtypeStruct(d.shape, BF16),
            jax.ShapeDtypeStruct((owners, nb, 128), BF16),
            jax.ShapeDtypeStruct((wdim, width), BF16 if later else F32),
        ],
        scratch_shapes=[pltpu.VMEM((wdim, width), F32)],
        input_output_aliases={4: 0, 5: 1} if later else {},
        compiler_params=pltpu.CompilerParams(vmem_limit_bytes=40 * MIB),
        cost_estimate=pl.CostEstimate(
            flops=4 * owners * part * wdim * width,
            bytes_accessed=owners * part * 2 * 1024,
            transcendentals=0,
        ),
        name="owner_backward",
    )(gu, gu, d, wd, *before)


def owner_split_body(*refs):
    *gx_refs, gat_ref, gbt_ref = refs
    narrow = jnp.concatenate([r[...] for r in gx_refs], axis=1).reshape(-1, 128).T
    gbt_ref[...] = narrow[0:64]
    gat_ref[...] = narrow[64:96]


def owner_split(gus, group=8):
    owners, _, full = gus[0].shape
    nb = sum(gu.shape[1] for gu in gus)
    total, rows = owners * nb, group * nb
    return pl.pallas_call(
        owner_split_body,
        grid=(owners // group,),
        in_specs=[
            pl.BlockSpec((group, gu.shape[1], 128), lambda i: (i, 0, full // 128 - 1)) for gu in gus
        ],
        out_specs=[
            pl.BlockSpec((32, rows), lambda i: (0, i)),
            pl.BlockSpec((64, rows), lambda i: (0, i)),
        ],
        out_shape=[
            jax.ShapeDtypeStruct((32, total), BF16),
            jax.ShapeDtypeStruct((64, total), BF16),
        ],
        compiler_params=pltpu.CompilerParams(vmem_limit_bytes=40 * MIB),
        cost_estimate=pl.CostEstimate(flops=0, bytes_accessed=total * 2 * 224, transcendentals=0),
        name="owner_split",
    )(*gus)


def exchange(x):
    return lax.all_to_all(x, PLANE, split_axis=0, concat_axis=0, tiled=True)


def shift(x, axis, k):
    n = lax.axis_size(axis)
    return lax.ppermute(x, axis, [(i, (i + k) % n) for i in range(n)])


def add(*parts):
    total = parts[0].astype(F32)
    for p in parts[1:]:
        total = total + p.astype(F32)
    return total


def turn_features(w, y):
    blocks = w.reshape(w.shape[0], 4, 128)
    order = lax.rem(y - jnp.arange(4) + 4, 4)
    return jnp.take(blocks, order, axis=1).reshape(w.shape)


def gather_axis(part, axis):
    return jnp.concatenate([part, shift(part, axis, 1), shift(part, axis, 2), shift(part, axis, -1)])


def gather_quarters(part):
    below, above = shift(part, "y", 1), shift(part, "y", -1)
    far = jnp.concatenate([shift(below[:8], "y", 1), shift(above[8:], "y", -1)])
    own = (part, below, far, above)
    return own + tuple(shift(p, "c", 1) for p in own)


def scatter_far(own, other):
    s = add(own[2], shift(other[2], "c", 1)).astype(BF16)
    from_above, from_below = shift(s[:8], "y", -1), shift(s[8:], "y", 1)
    s = [add(own[r], shift(other[r], "c", 1)) for r in (0, 1, 3)]
    down = jnp.concatenate([add(s[1][:8], from_above), s[1][8:]]).astype(BF16)
    up = jnp.concatenate([s[2][:8], add(s[2][8:], from_below)]).astype(BF16)
    return s[0], down, up


def scatter_near(own, down, up):
    return add(own, shift(down, "y", -1), shift(up, "y", 1)).astype(BF16)


def scatter_axis(part, axis):
    n = part.shape[0] // 4
    return (part[:n],) + tuple(shift(part[k * n : (k + 1) * n], axis, -k) for k in (1, 2, 3))


def on_device(
    pooled_a, pooled_b, pooled_c, pooled_d, proj_a, proj_b, proj_c, proj_d,
    slot_table, norm_gain, grad_gram,
):
    total = pooled_a.shape[0]
    nb = grad_gram.shape[0]
    owners = total // nb
    y = lax.axis_index("y")
    at = jnp.stack([lax.axis_index("z"), lax.axis_index("x"), lax.axis_index("c")]).astype(jnp.int32)
    wd = turn_features(proj_d[0], y)
    gain = turn_features(norm_gain[None], y)
    d = pooled_d[:, 0]
    part = jnp.concatenate([proj_c[0], proj_b[0], proj_a[0]], axis=0)
    part = gather_axis(lax.dynamic_slice_in_dim(part, y * 128, 128, axis=1)[None], "x")
    wd, part = lax.optimization_barrier((wd, part))
    part = gather_axis(part, "z")
    us = owner_forward(
        pooled_a.transpose(1, 2, 0)[0], pooled_b.transpose(1, 2, 0)[0], pooled_c[:, 0], d, wd, nb
    )
    u0, u1 = us
    start = u0.shape[1]
    u0, part = lax.optimization_barrier((u0, part))
    ws = gather_quarters(part)
    u0 = exchange(u0)
    u1, u0, ws = lax.optimization_barrier((u1, u0, ws))
    u1 = exchange(u1)
    gu0, *gws = middle(0, at, slot_table, gain, u0, ws, grad_gram, [])
    gu0 = exchange(gu0)
    gu1, *gws = middle(start, at, slot_table, gain, u1, ws, grad_gram, gws)
    own, down, up = scatter_far(gws[:4], gws[4:])
    gu1, down, up = lax.optimization_barrier((gu1, down, up))
    gu1 = exchange(gu1)
    d = d.reshape(owners, nb, -1)
    gd, gc, gwd = owner_backward(0, gu0, d, wd)
    part = scatter_near(own, down, up)
    gd, gc, gwd, part = lax.optimization_barrier((gd, gc, gwd, part))
    gd, gc, gwd = owner_backward(start, gu1, d, wd, (gd, gc, gwd))
    gd, gc = gd.reshape(total, -1), gc.reshape(total, -1)
    q = [gwd[:, r * 128 : (r + 1) * 128] for r in range(4)]
    q = [q[0]] + [shift(q[r], "y", -r) for r in (1, 2, 3)]
    pieces, _ = lax.optimization_barrier((scatter_axis(part, "z"), gwd))
    pieces = scatter_axis(add(*pieces).astype(BF16), "x")
    gat, gbt = owner_split((gu0, gu1))
    pieces, q, gat, gbt = lax.optimization_barrier((pieces, q, gat, gbt))
    scale = 1.0 / np.sqrt(total * lax.axis_size("y")).astype(np.float32)
    gw = add(*pieces)[0] * scale
    gwd = add(*q) * scale
    return (
        gat.T[:, None],
        gbt.T[:, None],
        gc[:, None],
        gd[:, None],
        gw[192:224][None],
        gw[128:192][None],
        gw[0:128][None],
        gwd[None],
    )


def solution(mesh):
    fine = Mesh(np.array(mesh.devices).reshape(4, 4, 4, 2), ("y", "z", "x", "c"))
    pooled = P("y", PLANE, None)
    weight = P(PLANE, None, None)
    in_specs = (pooled,) * 4 + (weight,) * 4 + (P(), P(), P(("y",) + PLANE, None, None))
    out_specs = (pooled,) * 4 + (P(PLANE, None, "y"),) * 4
    return jax.shard_map(
        on_device, mesh=fine, in_specs=in_specs, out_specs=out_specs, check_vma=False
    )
```

```python
import jax
import jax.numpy as jnp
import numpy as np
from jax import lax
from jax.experimental import pallas as pl
from jax.experimental.pallas import tpu as pltpu
from jax.sharding import Mesh, PartitionSpec as P

F32 = jnp.float32
BF16 = jnp.bfloat16
PLANE = ("z", "x", "c")
MIB = 1024 * 1024
ROWS = 224
GROUP = 8
UNROLL = 8
PARTS = (5, 3)


def dot(a, b, dims=((1,), (0,))):
    return lax.dot_general(a, b, (dims, ((), ())), preferred_element_type=F32)


def owner_forward_body(at_ref, bt_ref, c_ref, d_ref, wd_ref, *u_refs):
    rows, width = c_ref.shape[0], wd_ref.shape[1]
    narrow = jnp.concatenate(
        [bt_ref[...], at_ref[...], jnp.zeros((32, rows), BF16)], axis=0
    )
    group = u_refs[0].shape[0]

    def place(value, start, stop):
        value = value.reshape(group, rows // group, stop - start)
        first = 0
        for u_ref in u_refs:
            part = u_ref.shape[1]
            u_ref[:, :, start:stop] = value[:, first : first + part]
            first += part

    place(dot(d_ref[...], wd_ref[...]).astype(BF16), 0, width)
    place(c_ref[...], width, width + 128)
    place(narrow.T, width + 128, width + 256)


def owner_forward(at, bt, c, d, wd, nb, rows=512):
    total, width = c.shape[0], wd.shape[1]
    parts = [nb * n // sum(PARTS) for n in PARTS]
    return pl.pallas_call(
        owner_forward_body,
        grid=(total // rows,),
        in_specs=[
            pl.BlockSpec((at.shape[0], rows), lambda i: (0, i)),
            pl.BlockSpec((bt.shape[0], rows), lambda i: (0, i)),
            pl.BlockSpec((rows, c.shape[1]), lambda i: (i, 0)),
            pl.BlockSpec((rows, d.shape[1]), lambda i: (i, 0)),
            pl.BlockSpec(wd.shape, lambda i: (0, 0)),
        ],
        out_specs=[pl.BlockSpec((rows // nb, n, width + 256), lambda i: (i, 0, 0)) for n in parts],
        out_shape=[pltpu.HBM((total // nb, n, width + 256), BF16) for n in parts],
        compiler_params=pltpu.CompilerParams(vmem_limit_bytes=40 * MIB),
        cost_estimate=pl.CostEstimate(
            flops=2 * total * 256 * width, bytes_accessed=total * 2 * (480 + 768), transcendentals=0
        ),
        name="owner_forward",
    )(at, bt, c, d, wd)


def padded_weights(w):
    zeros = lambda n: jnp.zeros((n, w.shape[1]), w.dtype)
    wc = w[0:128]
    wb = jnp.concatenate([w[128:192], zeros(64)], axis=0)
    wa = jnp.concatenate([zeros(64), w[192:224], zeros(32)], axis=0)
    return wa, wb, wc


def middle_body(
    steps, later, at_ref, table_ref, gain_ref, pd_ref, x_ref, w00, w01, w02, w03, w10, w11, w12, w13,
    g_ref, *refs,
):
    before = (refs[0:4], refs[4:8])
    gu_ref, v00, v01, v02, v03, v10, v11, v12, v13, scr, nrm, acc = refs[8 if later else 0 :]
    i = pl.program_id(0)
    nb = x_ref.shape[1]
    ns = nb + 1
    width = gain_ref.shape[1]
    lanes = range(width // 128)
    plane = 128 * ns
    weights = ((w00, w01, w02, w03), (w10, w11, w12, w13))
    weight_grads = ((v00, v01, v02, v03), (v10, v11, v12, v13))
    z, x, core = at_ref[0], at_ref[1], at_ref[2]

    def put(slot, value):
        start = table_ref[slot] * ns
        for q in lanes:
            scr[pl.ds(q * plane + start, nb), :] = value[:, q * 128 : (q + 1) * 128]

    def take(slot):
        start = table_ref[slot] * ns
        pieces = [scr[pl.ds(q * plane + start, nb), :].astype(BF16) for q in lanes]
        return jnp.concatenate(pieces, axis=1)

    def strided(q, r, b):
        return pl.ds(q * plane + r * ns + b, 32, stride=ns)

    def tables(dz):
        zabs = lax.rem(z - dz + 4, 4)
        for dx in range(4):
            for side in range(2):
                t = lax.rem(x - dx + 4, 4) * 2 + lax.rem(core + side, 2)
                w = jnp.concatenate([weights[side][q][dx] for q in lanes], axis=1)
                yield dx, side, t, zabs * GROUP + t, padded_weights(w)

    @pl.when(i < 4)
    def _():
        for dx, side, t, j, (wa, wb, wc) in tables(i):
            xc = x_ref[t, :, 0:128]
            xn = x_ref[t, :, 128:256]
            put(j, dot(xn, wa).astype(BF16).astype(F32))
            put(32 + j, dot(xn, wb).astype(BF16).astype(F32))
            put(64 + j, dot(xc, wc).astype(BF16).astype(F32))
            put(96 + j, pd_ref[t].astype(F32))

    @pl.when((i >= 4) & (i < 4 + steps))
    def _():
        per = g_ref.shape[0]
        gain = gain_ref[...]
        scaled = gain * (1.0 / np.sqrt(width).astype(np.float32))
        base = (i - 4) * per

        def one(s, u):
            b = base + s
            for r in range(0, 128, 32):
                pf = jnp.concatenate([scr[strided(q, r, b), :] for q in lanes], axis=1)
                inv = lax.rsqrt(jnp.sum(pf * pf, axis=1, keepdims=True) * (1.0 / width) + 1e-06)
                nrm[u, r : r + 32, :] = (pf * inv * gain).astype(BF16)
            g = g_ref[s]
            n = nrm[u]
            acc[u] = dot(jnp.concatenate([g, g.T], axis=1), jnp.concatenate([n, n], axis=0))
            for r in range(0, 128, 32):
                pf = jnp.concatenate([scr[strided(q, r, b), :] for q in lanes], axis=1)
                h = acc[u, r : r + 32, :] * scaled
                inv = lax.rsqrt(jnp.sum(pf * pf, axis=1, keepdims=True) * (1.0 / width) + 1e-06)
                m = jnp.sum(pf * h, axis=1, keepdims=True) * (1.0 / width)
                out = inv * h - pf * (inv * inv * inv * m)
                for q in lanes:
                    scr[strided(q, r, b), :] = out[:, q * 128 : (q + 1) * 128]

        def several(v, carry):
            for u in range(UNROLL):
                one(v * UNROLL + u, u)
            return carry

        lax.fori_loop(0, per // UNROLL, several, 0)

    @pl.when(i >= 4 + steps)
    def _():
        last, first = ((1,), (1,)), ((0,), (0,))
        for dx, side, t, j, (wa, wb, wc) in tables(i - 4 - steps):
            xc = x_ref[t, :, 0:128]
            xn = x_ref[t, :, 128:256]
            ga, gb, gc = take(j), take(32 + j), take(64 + j)
            gu_ref[t, :, 0:width] = take(96 + j)
            gu_ref[t, :, width : width + 128] = dot(gc, wc, last).astype(BF16)
            gu_ref[t, :, width + 128 : width + 256] = (
                dot(ga, wa, last) + dot(gb, wb, last)
            ).astype(BF16)
            vc = dot(xc, gc, first)
            vb = dot(xn, gb, first)[0:64]
            va = dot(xn, ga, first)[64:96]
            for q in lanes:
                for value, rows in ((vc, slice(0, 128)), (vb, slice(128, 192)), (va, slice(192, 224))):
                    piece = value[:, q * 128 : (q + 1) * 128]
                    if later:
                        piece = piece + before[side][q][dx, rows, :].astype(F32)
                    weight_grads[side][q][dx, rows, :] = piece.astype(BF16)


def middle(start, at, table, gain, u, ws, g, before, per=16):
    ntab, nb, full = u.shape
    width = gain.shape[1]
    steps = nb // per

    def turn(i):
        return jnp.where(i < 4, i, jnp.where(i < 4 + steps, 3, i - 4 - steps))

    def by_table(i, at):
        return lax.rem(at[0] - turn(i) + 4, 4)

    def forward_only(i, at):
        return lax.rem(at[0] - jnp.minimum(i, 3) + 4, 4)

    def late(i):
        return jnp.maximum(i - 4 - steps, 0)

    def backward_only(i, at):
        return lax.rem(at[0] - late(i) + 4, 4)

    weight_in = pl.BlockSpec((4, ROWS, 128), lambda i, at, tb: (turn(i), 0, 0))
    weight_out = pl.BlockSpec((4, ROWS, 128), lambda i, at, tb: (late(i), 0, 0))
    return pl.pallas_call(
        lambda *refs: middle_body(steps, len(before) > 0, *refs),
        grid_spec=pltpu.PrefetchScalarGridSpec(
            num_scalar_prefetch=2,
            grid=(8 + steps,),
            in_specs=[
                pl.BlockSpec((1, width), lambda i, at, tb: (0, 0)),
                pl.BlockSpec((GROUP, nb, width), lambda i, at, tb: (forward_only(i, at), 0, 0)),
                pl.BlockSpec(
                    (GROUP, nb, 256), lambda i, at, tb: (by_table(i, at), 0, width // 256)
                ),
            ]
            + [weight_in] * 8
            + [
                pl.BlockSpec(
                    (per, 128, 128),
                    lambda i, at, tb: (start // per + jnp.clip(i - 4, 0, steps - 1), 0, 0),
                ),
            ]
            + [weight_out] * len(before),
            out_specs=[
                pl.BlockSpec((GROUP, nb, full), lambda i, at, tb: (backward_only(i, at), 0, 0)),
            ]
            + [weight_out] * 8,
            scratch_shapes=[
                pltpu.VMEM((width * (nb + 1), 128), F32),
                pltpu.VMEM((UNROLL, 128, width), BF16),
                pltpu.VMEM((UNROLL, 128, width), F32),
            ],
        ),
        out_shape=[pltpu.HBM((ntab, nb, full), BF16)]
        + [jax.ShapeDtypeStruct((16, ROWS, 128), BF16)] * 8,
        compiler_params=pltpu.CompilerParams(vmem_limit_bytes=58 * MIB),
        cost_estimate=pl.CostEstimate(
            flops=nb * 10**8, bytes_accessed=35 * 10**6, transcendentals=0
        ),
        name="middle",
    )(at, table, gain, u, u, *ws, g, *before)


def owner_backward_body(later, gp_ref, gx_ref, d_ref, wd_ref, *refs):
    gd_ref, gc_ref, gw_ref, acc = refs[-4:]
    i = pl.program_id(0)
    owners, part, wdim = d_ref.shape
    gp = gp_ref[...].reshape(owners * part, -1)
    gd = dot(gp, wd_ref[...], ((1,), (1,))).astype(BF16)
    gd_ref[...] = gd.reshape(owners, part, wdim)
    gc_ref[...] = gx_ref[...]

    @pl.when(i == 0)
    def _():
        acc[...] = refs[2][...] if later else jnp.zeros_like(acc)

    acc[...] += dot(d_ref[...].reshape(owners * part, wdim), gp, ((0,), (0,)))

    @pl.when(i == pl.num_programs(0) - 1)
    def _():
        gw_ref[...] = acc[...].astype(gw_ref.dtype)


def owner_backward(start, gu, d, wd, before=(), per=16):
    owners, nb, wdim = d.shape
    width = wd.shape[1]
    part = gu.shape[1]
    later = len(before) > 0
    whole = pl.BlockSpec((wdim, width), lambda i: (0, 0))
    d_spec = pl.BlockSpec((owners, per, wdim), lambda i: (0, start // per + i, 0))
    c_spec = pl.BlockSpec((owners, per, 128), lambda i: (0, start // per + i, 0))
    in_specs = [
        pl.BlockSpec((owners, per, width), lambda i: (0, i, 0)),
        pl.BlockSpec((owners, per, 128), lambda i: (0, i, width // 128)),
        d_spec,
        whole,
    ]
    if later:
        in_specs += [pl.BlockSpec(memory_space=pl.ANY)] * 2 + [whole]
    return pl.pallas_call(
        lambda *refs: owner_backward_body(later, *refs),
        grid=(part // per,),
        in_specs=in_specs,
        out_specs=[d_spec, c_spec, whole],
        out_shape=[
            jax.ShapeDtypeStruct(d.shape, BF16),
            jax.ShapeDtypeStruct((owners, nb, 128), BF16),
            jax.ShapeDtypeStruct((wdim, width), BF16 if later else F32),
        ],
        scratch_shapes=[pltpu.VMEM((wdim, width), F32)],
        input_output_aliases={4: 0, 5: 1} if later else {},
        compiler_params=pltpu.CompilerParams(vmem_limit_bytes=40 * MIB),
        cost_estimate=pl.CostEstimate(
            flops=4 * owners * part * wdim * width,
            bytes_accessed=owners * part * 2 * 1024,
            transcendentals=0,
        ),
        name="owner_backward",
    )(gu, gu, d, wd, *before)


def owner_split_body(*refs):
    *gx_refs, gat_ref, gbt_ref = refs
    narrow = jnp.concatenate([r[...] for r in gx_refs], axis=1).reshape(-1, 128).T
    gbt_ref[...] = narrow[0:64]
    gat_ref[...] = narrow[64:96]


def owner_split(gus, group=8):
    owners, _, full = gus[0].shape
    nb = sum(gu.shape[1] for gu in gus)
    total, rows = owners * nb, group * nb
    return pl.pallas_call(
        owner_split_body,
        grid=(owners // group,),
        in_specs=[
            pl.BlockSpec((group, gu.shape[1], 128), lambda i: (i, 0, full // 128 - 1)) for gu in gus
        ],
        out_specs=[
            pl.BlockSpec((32, rows), lambda i: (0, i)),
            pl.BlockSpec((64, rows), lambda i: (0, i)),
        ],
        out_shape=[
            jax.ShapeDtypeStruct((32, total), BF16),
            jax.ShapeDtypeStruct((64, total), BF16),
        ],
        compiler_params=pltpu.CompilerParams(vmem_limit_bytes=40 * MIB),
        cost_estimate=pl.CostEstimate(flops=0, bytes_accessed=total * 2 * 224, transcendentals=0),
        name="owner_split",
    )(*gus)


def exchange(x):
    return lax.all_to_all(x, PLANE, split_axis=0, concat_axis=0, tiled=True)


def shift(x, axis, k):
    n = lax.axis_size(axis)
    return lax.ppermute(x, axis, [(i, (i + k) % n) for i in range(n)])


def add(*parts):
    total = parts[0].astype(F32)
    for p in parts[1:]:
        total = total + p.astype(F32)
    return total


def turn_features(w, y):
    blocks = w.reshape(w.shape[0], 4, 128)
    order = lax.rem(y - jnp.arange(4) + 4, 4)
    return jnp.take(blocks, order, axis=1).reshape(w.shape)


def cross_shift(x, k, swap):
    moves = []
    for z in range(4):
        for xx in range(4):
            for c in range(2):
                along_x = (c == 0) != swap
                to = (z, (xx + k) % 4) if along_x else ((z + k) % 4, xx)
                moves.append((z * 8 + xx * 2 + c, to[0] * 8 + to[1] * 2 + c))
    return lax.ppermute(x, PLANE, moves)


def gather_plane(part):
    part = jnp.concatenate([part] + [cross_shift(part, k, False) for k in (1, 2, 3)])
    pieces = [part] + [cross_shift(part, k, True) for k in (1, 2, 3)]
    first = lax.axis_index("c") == 0
    pieces = jnp.where(first, jnp.stack(pieces), jnp.stack(pieces, axis=1))
    return pieces.reshape((16,) + part.shape[1:])


def scatter_outer(part):
    part = part.reshape((4, 4) + part.shape[1:])
    part = jnp.where(lax.axis_index("c") == 0, part, part.swapaxes(0, 1))
    return [part[0]] + [cross_shift(part[k], -k, True) for k in (1, 2, 3)]


def scatter_inner(part):
    return [part[0]] + [cross_shift(part[k], -k, False) for k in (1, 2, 3)]


def gather_quarters(part):
    below, above = shift(part, "y", 1), shift(part, "y", -1)
    far = jnp.concatenate([shift(below[:8], "y", 1), shift(above[8:], "y", -1)])
    own = (part, below, far, above)
    return own + tuple(shift(p, "c", 1) for p in own)


def scatter_far(own, other):
    s = add(own[2], shift(other[2], "c", 1)).astype(BF16)
    from_above, from_below = shift(s[:8], "y", -1), shift(s[8:], "y", 1)
    s = [add(own[r], shift(other[r], "c", 1)) for r in (0, 1, 3)]
    down = jnp.concatenate([add(s[1][:8], from_above), s[1][8:]]).astype(BF16)
    up = jnp.concatenate([s[2][:8], add(s[2][8:], from_below)]).astype(BF16)
    return s[0], down, up


def scatter_near(own, down, up):
    return add(own, shift(down, "y", -1), shift(up, "y", 1)).astype(BF16)


def on_device(
    pooled_a, pooled_b, pooled_c, pooled_d, proj_a, proj_b, proj_c, proj_d,
    slot_table, norm_gain, grad_gram,
):
    total = pooled_a.shape[0]
    nb = grad_gram.shape[0]
    owners = total // nb
    y = lax.axis_index("y")
    at = jnp.stack([lax.axis_index("z"), lax.axis_index("x"), lax.axis_index("c")]).astype(jnp.int32)
    wd = turn_features(proj_d[0], y)
    gain = turn_features(norm_gain[None], y)
    d = pooled_d[:, 0]
    part = jnp.concatenate([proj_c[0], proj_b[0], proj_a[0]], axis=0)
    part = gather_plane(lax.dynamic_slice_in_dim(part, y * 128, 128, axis=1)[None])
    us = owner_forward(
        pooled_a.transpose(1, 2, 0)[0], pooled_b.transpose(1, 2, 0)[0], pooled_c[:, 0], d, wd, nb
    )
    u0, u1 = us
    start = u0.shape[1]
    u0, part = lax.optimization_barrier((u0, part))
    ws = gather_quarters(part)
    u0 = exchange(u0)
    u1, u0, ws = lax.optimization_barrier((u1, u0, ws))
    u1 = exchange(u1)
    gu0, *gws = middle(0, at, slot_table, gain, u0, ws, grad_gram, [])
    gu0 = exchange(gu0)
    gu1, *gws = middle(start, at, slot_table, gain, u1, ws, grad_gram, gws)
    own, down, up = scatter_far(gws[:4], gws[4:])
    gu1, down, up = lax.optimization_barrier((gu1, down, up))
    gu1 = exchange(gu1)
    d = d.reshape(owners, nb, -1)
    gd, gc, gwd = owner_backward(0, gu0, d, wd)
    part = scatter_near(own, down, up)
    gd, gc, gwd, part = lax.optimization_barrier((gd, gc, gwd, part))
    gd, gc, gwd = owner_backward(start, gu1, d, wd, (gd, gc, gwd))
    gd, gc = gd.reshape(total, -1), gc.reshape(total, -1)
    q = [gwd[:, r * 128 : (r + 1) * 128] for r in range(4)]
    q = [q[0]] + [shift(q[r], "y", -r) for r in (1, 2, 3)]
    pieces, _ = lax.optimization_barrier((scatter_outer(part), gwd))
    pieces = scatter_inner(add(*pieces).astype(BF16))
    gat, gbt = owner_split((gu0, gu1))
    pieces, q, gat, gbt = lax.optimization_barrier((pieces, q, gat, gbt))
    scale = 1.0 / np.sqrt(total * lax.axis_size("y")).astype(np.float32)
    gw = lambda start, stop: add(*[p[None, start:stop] for p in pieces]) * scale
    gwd = add(*q) * scale
    return (
        gat.T[:, None],
        gbt.T[:, None],
        gc[:, None],
        gd[:, None],
        gw(192, 224),
        gw(128, 192),
        gw(0, 128),
        gwd[None],
    )


def solution(mesh):
    fine = Mesh(np.array(mesh.devices).reshape(4, 4, 4, 2), ("y", "z", "x", "c"))
    pooled = P("y", PLANE, None)
    weight = P(PLANE, None, None)
    in_specs = (pooled,) * 4 + (weight,) * 4 + (P(), P(), P(("y",) + PLANE, None, None))
    out_specs = (pooled,) * 4 + (P(PLANE, None, "y"),) * 4
    return jax.shard_map(
        on_device, mesh=fine, in_specs=in_specs, out_specs=out_specs, check_vma=False
    )
```

```python
import jax
import jax.numpy as jnp
import numpy as np
from jax import lax
from jax.experimental import pallas as pl
from jax.experimental.pallas import tpu as pltpu
from jax.sharding import Mesh, PartitionSpec as P

F32 = jnp.float32
BF16 = jnp.bfloat16
PLANE = ("z", "x", "c")
MIB = 1024 * 1024
ROWS = 224
GROUP = 8
UNROLL = 4
PARTS = (5, 3)


def dot(a, b, dims=((1,), (0,))):
    return lax.dot_general(a, b, (dims, ((), ())), preferred_element_type=F32)


def owner_forward_body(at_ref, bt_ref, c_ref, d_ref, wd_ref, *u_refs):
    rows, width = c_ref.shape[0], wd_ref.shape[1]
    narrow = jnp.concatenate(
        [bt_ref[...], at_ref[...], jnp.zeros((32, rows), BF16)], axis=0
    )
    group = u_refs[0].shape[0]

    def place(value, start, stop):
        value = value.reshape(group, rows // group, stop - start)
        first = 0
        for u_ref in u_refs:
            part = u_ref.shape[1]
            u_ref[:, :, start:stop] = value[:, first : first + part]
            first += part

    place(dot(d_ref[...], wd_ref[...]).astype(BF16), 0, width)
    place(c_ref[...], width, width + 128)
    place(narrow.T, width + 128, width + 256)


def owner_forward(at, bt, c, d, wd, nb, rows=512):
    total, width = c.shape[0], wd.shape[1]
    parts = [nb * n // sum(PARTS) for n in PARTS]
    return pl.pallas_call(
        owner_forward_body,
        grid=(total // rows,),
        in_specs=[
            pl.BlockSpec((at.shape[0], rows), lambda i: (0, i)),
            pl.BlockSpec((bt.shape[0], rows), lambda i: (0, i)),
            pl.BlockSpec((rows, c.shape[1]), lambda i: (i, 0)),
            pl.BlockSpec((rows, d.shape[1]), lambda i: (i, 0)),
            pl.BlockSpec(wd.shape, lambda i: (0, 0)),
        ],
        out_specs=[pl.BlockSpec((rows // nb, n, width + 256), lambda i: (i, 0, 0)) for n in parts],
        out_shape=[pltpu.HBM((total // nb, n, width + 256), BF16) for n in parts],
        compiler_params=pltpu.CompilerParams(vmem_limit_bytes=40 * MIB),
        cost_estimate=pl.CostEstimate(
            flops=2 * total * 256 * width, bytes_accessed=total * 2 * (480 + 768), transcendentals=0
        ),
        name="owner_forward",
    )(at, bt, c, d, wd)


def padded_weights(w):
    zeros = lambda n: jnp.zeros((n, w.shape[1]), w.dtype)
    wc = w[0:128]
    wb = jnp.concatenate([w[128:192], zeros(64)], axis=0)
    wa = jnp.concatenate([zeros(64), w[192:224], zeros(32)], axis=0)
    return wa, wb, wc


def middle_body(
    steps, later, at_ref, table_ref, gain_ref, pd_ref, x_ref, w00, w01, w02, w03, w10, w11, w12, w13,
    g_ref, *refs,
):
    before = (refs[0:4], refs[4:8])
    gu_ref, v00, v01, v02, v03, v10, v11, v12, v13, scr, nrm, acc = refs[8 if later else 0 :]
    i = pl.program_id(0)
    nb = x_ref.shape[1]
    ns = nb + 1
    width = gain_ref.shape[1]
    lanes = range(width // 128)
    plane = 128 * ns
    weights = ((w00, w01, w02, w03), (w10, w11, w12, w13))
    weight_grads = ((v00, v01, v02, v03), (v10, v11, v12, v13))
    z, x, core = at_ref[0], at_ref[1], at_ref[2]

    def put(slot, value):
        start = table_ref[slot] * ns
        for q in lanes:
            scr[pl.ds(q * plane + start, nb), :] = value[:, q * 128 : (q + 1) * 128]

    def take(slot):
        start = table_ref[slot] * ns
        pieces = [scr[pl.ds(q * plane + start, nb), :].astype(BF16) for q in lanes]
        return jnp.concatenate(pieces, axis=1)

    def strided(q, r, b):
        return pl.ds(q * plane + r * ns + b, 32, stride=ns)

    def tables(dz):
        zabs = lax.rem(z - dz + 4, 4)
        for dx in range(4):
            for side in range(2):
                t = lax.rem(x - dx + 4, 4) * 2 + lax.rem(core + side, 2)
                w = jnp.concatenate([weights[side][q][dx] for q in lanes], axis=1)
                yield dx, side, t, zabs * GROUP + t, padded_weights(w)

    @pl.when(i < 4)
    def _():
        for dx, side, t, j, (wa, wb, wc) in tables(i):
            xc = x_ref[t, :, 0:128]
            xn = x_ref[t, :, 128:256]
            put(j, dot(xn, wa).astype(BF16).astype(F32))
            put(32 + j, dot(xn, wb).astype(BF16).astype(F32))
            put(64 + j, dot(xc, wc).astype(BF16).astype(F32))
            put(96 + j, pd_ref[t].astype(F32))

    @pl.when((i >= 4) & (i < 4 + steps))
    def _():
        per = g_ref.shape[0]
        gain = gain_ref[...]
        scaled = gain * (1.0 / np.sqrt(width).astype(np.float32))
        base = (i - 4) * per

        def one(s, u):
            b = base + s
            for r in range(0, 128, 32):
                pf = jnp.concatenate([scr[strided(q, r, b), :] for q in lanes], axis=1)
                inv = lax.rsqrt(jnp.sum(pf * pf, axis=1, keepdims=True) * (1.0 / width) + 1e-06)
                nrm[u, r : r + 32, :] = (pf * inv * gain).astype(BF16)
            g = g_ref[s]
            n = nrm[u]
            acc[u] = dot(jnp.concatenate([g, g.T], axis=1), jnp.concatenate([n, n], axis=0))
            for r in range(0, 128, 32):
                pf = jnp.concatenate([scr[strided(q, r, b), :] for q in lanes], axis=1)
                h = acc[u, r : r + 32, :] * scaled
                inv = lax.rsqrt(jnp.sum(pf * pf, axis=1, keepdims=True) * (1.0 / width) + 1e-06)
                m = jnp.sum(pf * h, axis=1, keepdims=True) * (1.0 / width)
                out = inv * h - pf * (inv * inv * inv * m)
                for q in lanes:
                    scr[strided(q, r, b), :] = out[:, q * 128 : (q + 1) * 128]

        def several(v, carry):
            for u in range(UNROLL):
                one(v * UNROLL + u, u)
            return carry

        lax.fori_loop(0, per // UNROLL, several, 0)

    @pl.when(i >= 4 + steps)
    def _():
        last, first = ((1,), (1,)), ((0,), (0,))
        for dx, side, t, j, (wa, wb, wc) in tables(i - 4 - steps):
            xc = x_ref[t, :, 0:128]
            xn = x_ref[t, :, 128:256]
            ga, gb, gc = take(j), take(32 + j), take(64 + j)
            gu_ref[t, :, 0:width] = take(96 + j)
            gu_ref[t, :, width : width + 128] = dot(gc, wc, last).astype(BF16)
            gu_ref[t, :, width + 128 : width + 256] = (
                dot(ga, wa, last) + dot(gb, wb, last)
            ).astype(BF16)
            vc = dot(xc, gc, first)
            vb = dot(xn, gb, first)[0:64]
            va = dot(xn, ga, first)[64:96]
            for q in lanes:
                for value, rows in ((vc, slice(0, 128)), (vb, slice(128, 192)), (va, slice(192, 224))):
                    piece = value[:, q * 128 : (q + 1) * 128]
                    if later:
                        piece = piece + before[side][q][dx, rows, :].astype(F32)
                    weight_grads[side][q][dx, rows, :] = piece.astype(BF16)


def middle(start, at, table, gain, u, ws, g, before, per=16):
    ntab, nb, full = u.shape
    width = gain.shape[1]
    steps = nb // per

    def turn(i):
        return jnp.where(i < 4, i, jnp.where(i < 4 + steps, 3, i - 4 - steps))

    def by_table(i, at):
        return lax.rem(at[0] - turn(i) + 4, 4)

    def forward_only(i, at):
        return lax.rem(at[0] - jnp.minimum(i, 3) + 4, 4)

    def late(i):
        return jnp.maximum(i - 4 - steps, 0)

    def backward_only(i, at):
        return lax.rem(at[0] - late(i) + 4, 4)

    weight_in = pl.BlockSpec((4, ROWS, 128), lambda i, at, tb: (turn(i), 0, 0))
    weight_out = pl.BlockSpec((4, ROWS, 128), lambda i, at, tb: (late(i), 0, 0))
    return pl.pallas_call(
        lambda *refs: middle_body(steps, len(before) > 0, *refs),
        grid_spec=pltpu.PrefetchScalarGridSpec(
            num_scalar_prefetch=2,
            grid=(8 + steps,),
            in_specs=[
                pl.BlockSpec((1, width), lambda i, at, tb: (0, 0)),
                pl.BlockSpec((GROUP, nb, width), lambda i, at, tb: (forward_only(i, at), 0, 0)),
                pl.BlockSpec(
                    (GROUP, nb, 256), lambda i, at, tb: (by_table(i, at), 0, width // 256)
                ),
            ]
            + [weight_in] * 8
            + [
                pl.BlockSpec(
                    (per, 128, 128),
                    lambda i, at, tb: (start // per + jnp.clip(i - 4, 0, steps - 1), 0, 0),
                ),
            ]
            + [weight_out] * len(before),
            out_specs=[
                pl.BlockSpec((GROUP, nb, full), lambda i, at, tb: (backward_only(i, at), 0, 0)),
            ]
            + [weight_out] * 8,
            scratch_shapes=[
                pltpu.VMEM((width * (nb + 1) + 128, 128), F32),
                pltpu.VMEM((UNROLL, 128, width), BF16),
                pltpu.VMEM((UNROLL, 128, width), F32),
            ],
        ),
        out_shape=[pltpu.HBM((ntab, nb, full), BF16)]
        + [jax.ShapeDtypeStruct((16, ROWS, 128), BF16)] * 8,
        compiler_params=pltpu.CompilerParams(vmem_limit_bytes=58 * MIB),
        cost_estimate=pl.CostEstimate(
            flops=nb * 10**8, bytes_accessed=35 * 10**6, transcendentals=0
        ),
        name="middle",
    )(at, table, gain, u, u, *ws, g, *before)


def owner_backward_body(later, gp_ref, gx_ref, d_ref, wd_ref, *refs):
    gd_ref, gc_ref, gw_ref, acc = refs[-4:]
    i = pl.program_id(0)
    owners, part, wdim = d_ref.shape
    gp = gp_ref[...].reshape(owners * part, -1)
    gd = dot(gp, wd_ref[...], ((1,), (1,))).astype(BF16)
    gd_ref[...] = gd.reshape(owners, part, wdim)
    gc_ref[...] = gx_ref[...]

    @pl.when(i == 0)
    def _():
        acc[...] = refs[2][...] if later else jnp.zeros_like(acc)

    acc[...] += dot(d_ref[...].reshape(owners * part, wdim), gp, ((0,), (0,)))

    @pl.when(i == pl.num_programs(0) - 1)
    def _():
        gw_ref[...] = acc[...].astype(gw_ref.dtype)


def owner_backward(start, gu, d, wd, before=(), per=16):
    owners, nb, wdim = d.shape
    width = wd.shape[1]
    part = gu.shape[1]
    later = len(before) > 0
    whole = pl.BlockSpec((wdim, width), lambda i: (0, 0))
    d_spec = pl.BlockSpec((owners, per, wdim), lambda i: (0, start // per + i, 0))
    c_spec = pl.BlockSpec((owners, per, 128), lambda i: (0, start // per + i, 0))
    in_specs = [
        pl.BlockSpec((owners, per, width), lambda i: (0, i, 0)),
        pl.BlockSpec((owners, per, 128), lambda i: (0, i, width // 128)),
        d_spec,
        whole,
    ]
    if later:
        in_specs += [pl.BlockSpec(memory_space=pl.ANY)] * 2 + [whole]
    return pl.pallas_call(
        lambda *refs: owner_backward_body(later, *refs),
        grid=(part // per,),
        in_specs=in_specs,
        out_specs=[d_spec, c_spec, whole],
        out_shape=[
            jax.ShapeDtypeStruct(d.shape, BF16),
            jax.ShapeDtypeStruct((owners, nb, 128), BF16),
            jax.ShapeDtypeStruct((wdim, width), BF16 if later else F32),
        ],
        scratch_shapes=[pltpu.VMEM((wdim, width), F32)],
        input_output_aliases={4: 0, 5: 1} if later else {},
        compiler_params=pltpu.CompilerParams(vmem_limit_bytes=40 * MIB),
        cost_estimate=pl.CostEstimate(
            flops=4 * owners * part * wdim * width,
            bytes_accessed=owners * part * 2 * 1024,
            transcendentals=0,
        ),
        name="owner_backward",
    )(gu, gu, d, wd, *before)


def owner_split_body(*refs):
    *gx_refs, gat_ref, gbt_ref = refs
    narrow = jnp.concatenate([r[...] for r in gx_refs], axis=1).reshape(-1, 128).T
    gbt_ref[...] = narrow[0:64]
    gat_ref[...] = narrow[64:96]


def owner_split(gus, group=8):
    owners, _, full = gus[0].shape
    nb = sum(gu.shape[1] for gu in gus)
    total, rows = owners * nb, group * nb
    return pl.pallas_call(
        owner_split_body,
        grid=(owners // group,),
        in_specs=[
            pl.BlockSpec((group, gu.shape[1], 128), lambda i: (i, 0, full // 128 - 1)) for gu in gus
        ],
        out_specs=[
            pl.BlockSpec((32, rows), lambda i: (0, i)),
            pl.BlockSpec((64, rows), lambda i: (0, i)),
        ],
        out_shape=[
            jax.ShapeDtypeStruct((32, total), BF16),
            jax.ShapeDtypeStruct((64, total), BF16),
        ],
        compiler_params=pltpu.CompilerParams(vmem_limit_bytes=40 * MIB),
        cost_estimate=pl.CostEstimate(flops=0, bytes_accessed=total * 2 * 224, transcendentals=0),
        name="owner_split",
    )(*gus)


def exchange(x):
    return lax.all_to_all(x, PLANE, split_axis=0, concat_axis=0, tiled=True)


def shift(x, axis, k):
    n = lax.axis_size(axis)
    return lax.ppermute(x, axis, [(i, (i + k) % n) for i in range(n)])


def add(*parts):
    total = parts[0].astype(F32)
    for p in parts[1:]:
        total = total + p.astype(F32)
    return total


def turn_features(w, y):
    blocks = w.reshape(w.shape[0], 4, 128)
    order = lax.rem(y - jnp.arange(4) + 4, 4)
    return jnp.take(blocks, order, axis=1).reshape(w.shape)


def cross_shift(x, k, swap):
    moves = []
    for z in range(4):
        for xx in range(4):
            for c in range(2):
                along_x = (c == 0) != swap
                to = (z, (xx + k) % 4) if along_x else ((z + k) % 4, xx)
                moves.append((z * 8 + xx * 2 + c, to[0] * 8 + to[1] * 2 + c))
    return lax.ppermute(x, PLANE, moves)


def gather_plane(part):
    part = jnp.concatenate([part] + [cross_shift(part, k, False) for k in (1, 2, 3)])
    pieces = [part] + [cross_shift(part, k, True) for k in (1, 2, 3)]
    first = lax.axis_index("c") == 0
    pieces = jnp.where(first, jnp.stack(pieces), jnp.stack(pieces, axis=1))
    return pieces.reshape((16,) + part.shape[1:])


def scatter_outer(part):
    part = part.reshape((4, 4) + part.shape[1:])
    part = jnp.where(lax.axis_index("c") == 0, part, part.swapaxes(0, 1))
    return [part[0]] + [cross_shift(part[k], -k, True) for k in (1, 2, 3)]


def scatter_inner(part):
    return [part[0]] + [cross_shift(part[k], -k, False) for k in (1, 2, 3)]


def gather_quarters(part):
    below, above = shift(part, "y", 1), shift(part, "y", -1)
    far = jnp.concatenate([shift(below[:8], "y", 1), shift(above[8:], "y", -1)])
    own = (part, below, far, above)
    return own + tuple(shift(p, "c", 1) for p in own)


def scatter_far(own, other):
    s = add(own[2], shift(other[2], "c", 1)).astype(BF16)
    from_above, from_below = shift(s[:8], "y", -1), shift(s[8:], "y", 1)
    s = [add(own[r], shift(other[r], "c", 1)) for r in (0, 1, 3)]
    down = jnp.concatenate([add(s[1][:8], from_above), s[1][8:]]).astype(BF16)
    up = jnp.concatenate([s[2][:8], add(s[2][8:], from_below)]).astype(BF16)
    return s[0], down, up


def scatter_near(own, down, up):
    return add(own, shift(down, "y", -1), shift(up, "y", 1)).astype(BF16)


def on_device(
    pooled_a, pooled_b, pooled_c, pooled_d, proj_a, proj_b, proj_c, proj_d,
    slot_table, norm_gain, grad_gram,
):
    total = pooled_a.shape[0]
    nb = grad_gram.shape[0]
    owners = total // nb
    y = lax.axis_index("y")
    at = jnp.stack([lax.axis_index("z"), lax.axis_index("x"), lax.axis_index("c")]).astype(jnp.int32)
    wd = turn_features(proj_d[0], y)
    gain = turn_features(norm_gain[None], y)
    d = pooled_d[:, 0]
    part = jnp.concatenate([proj_c[0], proj_b[0], proj_a[0]], axis=0)
    part = gather_plane(lax.dynamic_slice_in_dim(part, y * 128, 128, axis=1)[None])
    us = owner_forward(
        pooled_a.transpose(1, 2, 0)[0], pooled_b.transpose(1, 2, 0)[0], pooled_c[:, 0], d, wd, nb
    )
    u0, u1 = us
    start = u0.shape[1]
    u0, part = lax.optimization_barrier((u0, part))
    ws = gather_quarters(part)
    u0 = exchange(u0)
    u1, u0, ws = lax.optimization_barrier((u1, u0, ws))
    u1 = exchange(u1)
    gu0, *gws = middle(0, at, slot_table, gain, u0, ws, grad_gram, [])
    gu0 = exchange(gu0)
    gu1, *gws = middle(start, at, slot_table, gain, u1, ws, grad_gram, gws)
    own, down, up = scatter_far(gws[:4], gws[4:])
    gu1, down, up = lax.optimization_barrier((gu1, down, up))
    gu1 = exchange(gu1)
    d = d.reshape(owners, nb, -1)
    gd, gc, gwd = owner_backward(0, gu0, d, wd)
    part = scatter_near(own, down, up)
    gd, gc, gwd, part = lax.optimization_barrier((gd, gc, gwd, part))
    gd, gc, gwd = owner_backward(start, gu1, d, wd, (gd, gc, gwd))
    gd, gc = gd.reshape(total, -1), gc.reshape(total, -1)
    q = [gwd[:, r * 128 : (r + 1) * 128] for r in range(4)]
    q = [q[0]] + [shift(q[r], "y", -r) for r in (1, 2, 3)]
    pieces, _ = lax.optimization_barrier((scatter_outer(part), gwd))
    pieces = scatter_inner(add(*pieces).astype(BF16))
    gat, gbt = owner_split((gu0, gu1))
    pieces, q, gat, gbt = lax.optimization_barrier((pieces, q, gat, gbt))
    scale = 1.0 / np.sqrt(total * lax.axis_size("y")).astype(np.float32)
    gw = lambda start, stop: add(*[p[None, start:stop] for p in pieces]) * scale
    gwd = add(*q) * scale
    return (
        gat.T[:, None],
        gbt.T[:, None],
        gc[:, None],
        gd[:, None],
        gw(192, 224),
        gw(128, 192),
        gw(0, 128),
        gwd[None],
    )


def solution(mesh):
    fine = Mesh(np.array(mesh.devices).reshape(4, 4, 4, 2), ("y", "z", "x", "c"))
    pooled = P("y", PLANE, None)
    weight = P(PLANE, None, None)
    in_specs = (pooled,) * 4 + (weight,) * 4 + (P(), P(), P(("y",) + PLANE, None, None))
    out_specs = (pooled,) * 4 + (P(PLANE, None, "y"),) * 4
    return jax.shard_map(
        on_device, mesh=fine, in_specs=in_specs, out_specs=out_specs, check_vma=False
    )
```

```python
import jax
import jax.numpy as jnp
import numpy as np
from jax import lax
from jax.experimental import pallas as pl
from jax.experimental.pallas import tpu as pltpu
from jax.sharding import Mesh, PartitionSpec as P

F32 = jnp.float32
BF16 = jnp.bfloat16
PLANE = ("z", "x", "c")
MIB = 1024 * 1024
ROWS = 224
GROUP = 8
UNROLL = 4
PARTS = (5, 3)


def dot(a, b, dims=((1,), (0,))):
    return lax.dot_general(a, b, (dims, ((), ())), preferred_element_type=F32)


def owner_forward_body(at_ref, bt_ref, c_ref, d_ref, wd_ref, *u_refs):
    rows, width = c_ref.shape[0], wd_ref.shape[1]
    narrow = jnp.concatenate(
        [bt_ref[...], at_ref[...], jnp.zeros((32, rows), BF16)], axis=0
    )
    group = u_refs[0].shape[0]

    def place(value, start, stop):
        value = value.reshape(group, rows // group, stop - start)
        first = 0
        for u_ref in u_refs:
            part = u_ref.shape[1]
            u_ref[:, :, start:stop] = value[:, first : first + part]
            first += part

    place(dot(d_ref[...], wd_ref[...]).astype(BF16), 0, width)
    place(c_ref[...], width, width + 128)
    place(narrow.T, width + 128, width + 256)


def owner_forward(at, bt, c, d, wd, nb, rows=512):
    total, width = c.shape[0], wd.shape[1]
    parts = [nb * n // sum(PARTS) for n in PARTS]
    return pl.pallas_call(
        owner_forward_body,
        grid=(total // rows,),
        in_specs=[
            pl.BlockSpec((at.shape[0], rows), lambda i: (0, i)),
            pl.BlockSpec((bt.shape[0], rows), lambda i: (0, i)),
            pl.BlockSpec((rows, c.shape[1]), lambda i: (i, 0)),
            pl.BlockSpec((rows, d.shape[1]), lambda i: (i, 0)),
            pl.BlockSpec(wd.shape, lambda i: (0, 0)),
        ],
        out_specs=[pl.BlockSpec((rows // nb, n, width + 256), lambda i: (i, 0, 0)) for n in parts],
        out_shape=[pltpu.HBM((total // nb, n, width + 256), BF16) for n in parts],
        compiler_params=pltpu.CompilerParams(vmem_limit_bytes=40 * MIB),
        cost_estimate=pl.CostEstimate(
            flops=2 * total * 256 * width, bytes_accessed=total * 2 * (480 + 768), transcendentals=0
        ),
        name="owner_forward",
    )(at, bt, c, d, wd)


def padded_weights(w):
    zeros = lambda n: jnp.zeros((n, w.shape[1]), w.dtype)
    wc = w[0:128]
    wb = jnp.concatenate([w[128:192], zeros(64)], axis=0)
    wa = jnp.concatenate([zeros(64), w[192:224], zeros(32)], axis=0)
    return wa, wb, wc


def middle_body(
    steps, later, at_ref, table_ref, gain_ref, pd_ref, x_ref, w00, w01, w02, w03, w10, w11, w12, w13,
    g_ref, *refs,
):
    before = (refs[0:4], refs[4:8])
    gu_ref, v00, v01, v02, v03, v10, v11, v12, v13, scr, nrm, acc = refs[8 if later else 0 :]
    i = pl.program_id(0)
    nb = x_ref.shape[1]
    ns = nb + 1
    width = gain_ref.shape[1]
    lanes = range(width // 128)
    plane = 128 * ns
    weights = ((w00, w01, w02, w03), (w10, w11, w12, w13))
    weight_grads = ((v00, v01, v02, v03), (v10, v11, v12, v13))
    z, x, core = at_ref[0], at_ref[1], at_ref[2]

    def put(slot, value):
        start = table_ref[slot] * ns
        for q in lanes:
            scr[pl.ds(q * plane + start, nb), :] = value[:, q * 128 : (q + 1) * 128]

    def take(slot):
        start = table_ref[slot] * ns
        pieces = [scr[pl.ds(q * plane + start, nb), :].astype(BF16) for q in lanes]
        return jnp.concatenate(pieces, axis=1)

    def strided(q, r, b):
        return pl.ds(q * plane + r * ns + b, 32, stride=ns)

    def tables(dz):
        zabs = lax.rem(z - dz + 4, 4)
        for dx in range(4):
            for side in range(2):
                t = lax.rem(x - dx + 4, 4) * 2 + lax.rem(core + side, 2)
                w = jnp.concatenate([weights[side][q][dx] for q in lanes], axis=1)
                yield dx, side, t, zabs * GROUP + t, padded_weights(w)

    @pl.when(i < 4)
    def _():
        for dx, side, t, j, (wa, wb, wc) in tables(i):
            xc = x_ref[t, :, 0:128]
            xn = x_ref[t, :, 128:256]
            put(j, dot(xn, wa).astype(BF16).astype(F32))
            put(32 + j, dot(xn, wb).astype(BF16).astype(F32))
            put(64 + j, dot(xc, wc).astype(BF16).astype(F32))
            put(96 + j, pd_ref[t].astype(F32))

    @pl.when((i >= 4) & (i < 4 + steps))
    def _():
        per = g_ref.shape[0]
        gain = gain_ref[...]
        scaled = gain * (1.0 / np.sqrt(width).astype(np.float32))
        base = (i - 4) * per

        def one(s, u):
            b = base + s
            for r in range(0, 128, 32):
                pf = jnp.concatenate([scr[strided(q, r, b), :] for q in lanes], axis=1)
                inv = lax.rsqrt(jnp.sum(pf * pf, axis=1, keepdims=True) * (1.0 / width) + 1e-06)
                nrm[u, r : r + 32, :] = (pf * inv * gain).astype(BF16)
            g = g_ref[s]
            n = nrm[u]
            acc[u] = dot(jnp.concatenate([g, g.T], axis=1), jnp.concatenate([n, n], axis=0))
            for r in range(0, 128, 32):
                pf = jnp.concatenate([scr[strided(q, r, b), :] for q in lanes], axis=1)
                h = acc[u, r : r + 32, :] * scaled
                inv = lax.rsqrt(jnp.sum(pf * pf, axis=1, keepdims=True) * (1.0 / width) + 1e-06)
                m = jnp.sum(pf * h, axis=1, keepdims=True) * (1.0 / width)
                out = inv * h - pf * (inv * inv * inv * m)
                for q in lanes:
                    scr[strided(q, r, b), :] = out[:, q * 128 : (q + 1) * 128]

        def several(v, carry):
            for u in range(UNROLL):
                one(v * UNROLL + u, u)
            return carry

        lax.fori_loop(0, per // UNROLL, several, 0)

    @pl.when(i >= 4 + steps)
    def _():
        last, first = ((1,), (1,)), ((0,), (0,))
        for dx, side, t, j, (wa, wb, wc) in tables(i - 4 - steps):
            xc = x_ref[t, :, 0:128]
            xn = x_ref[t, :, 128:256]
            ga, gb, gc = take(j), take(32 + j), take(64 + j)
            gu_ref[t, :, 0:width] = take(96 + j)
            gu_ref[t, :, width : width + 128] = dot(gc, wc, last).astype(BF16)
            gu_ref[t, :, width + 128 : width + 256] = (
                dot(ga, wa, last) + dot(gb, wb, last)
            ).astype(BF16)
            vc = dot(xc, gc, first)
            vb = dot(xn, gb, first)[0:64]
            va = dot(xn, ga, first)[64:96]
            for q in lanes:
                for value, rows in ((vc, slice(0, 128)), (vb, slice(128, 192)), (va, slice(192, 224))):
                    piece = value[:, q * 128 : (q + 1) * 128]
                    if later:
                        piece = piece + before[side][q][dx, rows, :].astype(F32)
                    weight_grads[side][q][dx, rows, :] = piece.astype(BF16)


def middle(start, at, table, gain, u, ws, g, before, per=16):
    ntab, nb, full = u.shape
    width = gain.shape[1]
    steps = nb // per

    def turn(i):
        return jnp.where(i < 4, i, jnp.where(i < 4 + steps, 3, i - 4 - steps))

    def by_table(i, at):
        return lax.rem(at[0] - turn(i) + 4, 4)

    def forward_only(i, at):
        return lax.rem(at[0] - jnp.minimum(i, 3) + 4, 4)

    def late(i):
        return jnp.maximum(i - 4 - steps, 0)

    def backward_only(i, at):
        return lax.rem(at[0] - late(i) + 4, 4)

    weight_in = pl.BlockSpec((4, ROWS, 128), lambda i, at, tb: (turn(i), 0, 0))
    weight_out = pl.BlockSpec((4, ROWS, 128), lambda i, at, tb: (late(i), 0, 0))
    return pl.pallas_call(
        lambda *refs: middle_body(steps, len(before) > 0, *refs),
        grid_spec=pltpu.PrefetchScalarGridSpec(
            num_scalar_prefetch=2,
            grid=(8 + steps,),
            in_specs=[
                pl.BlockSpec((1, width), lambda i, at, tb: (0, 0)),
                pl.BlockSpec((GROUP, nb, width), lambda i, at, tb: (forward_only(i, at), 0, 0)),
                pl.BlockSpec(
                    (GROUP, nb, 256), lambda i, at, tb: (by_table(i, at), 0, width // 256)
                ),
            ]
            + [weight_in] * 8
            + [
                pl.BlockSpec(
                    (per, 128, 128),
                    lambda i, at, tb: (start // per + jnp.clip(i - 4, 0, steps - 1), 0, 0),
                ),
            ]
            + [weight_out] * len(before),
            out_specs=[
                pl.BlockSpec((GROUP, nb, full), lambda i, at, tb: (backward_only(i, at), 0, 0)),
            ]
            + [weight_out] * 8,
            scratch_shapes=[
                pltpu.VMEM((width * (nb + 1) + 128, 128), F32),
                pltpu.VMEM((UNROLL, 128, width), BF16),
                pltpu.VMEM((UNROLL, 128, width), F32),
            ],
        ),
        out_shape=[pltpu.HBM((ntab, nb, full), BF16)]
        + [jax.ShapeDtypeStruct((16, ROWS, 128), BF16)] * 8,
        compiler_params=pltpu.CompilerParams(vmem_limit_bytes=62 * MIB),
        cost_estimate=pl.CostEstimate(
            flops=nb * 10**8, bytes_accessed=35 * 10**6, transcendentals=0
        ),
        name="middle",
    )(at, table, gain, u, u, *ws, g, *before)


def owner_backward_body(later, gp_ref, gx_ref, d_ref, wd_ref, *refs):
    gd_ref, gc_ref, gw_ref, acc = refs[-4:]
    i = pl.program_id(0)
    owners, part, wdim = d_ref.shape
    gp = gp_ref[...].reshape(owners * part, -1)
    gd = dot(gp, wd_ref[...], ((1,), (1,))).astype(BF16)
    gd_ref[...] = gd.reshape(owners, part, wdim)
    gc_ref[...] = gx_ref[...]

    @pl.when(i == 0)
    def _():
        acc[...] = refs[2][...] if later else jnp.zeros_like(acc)

    acc[...] += dot(d_ref[...].reshape(owners * part, wdim), gp, ((0,), (0,)))

    @pl.when(i == pl.num_programs(0) - 1)
    def _():
        gw_ref[...] = acc[...].astype(gw_ref.dtype)


def owner_backward(start, gu, d, wd, before=(), per=16):
    owners, nb, wdim = d.shape
    width = wd.shape[1]
    part = gu.shape[1]
    d = pltpu.with_memory_space_constraint(d, pltpu.HBM)
    later = len(before) > 0
    whole = pl.BlockSpec((wdim, width), lambda i: (0, 0))
    d_spec = pl.BlockSpec((owners, per, wdim), lambda i: (0, start // per + i, 0))
    c_spec = pl.BlockSpec((owners, per, 128), lambda i: (0, start // per + i, 0))
    in_specs = [
        pl.BlockSpec((owners, per, width), lambda i: (0, i, 0)),
        pl.BlockSpec((owners, per, 128), lambda i: (0, i, width // 128)),
        d_spec,
        whole,
    ]
    if later:
        in_specs += [pl.BlockSpec(memory_space=pl.ANY)] * 2 + [whole]
    return pl.pallas_call(
        lambda *refs: owner_backward_body(later, *refs),
        grid=(part // per,),
        in_specs=in_specs,
        out_specs=[d_spec, c_spec, whole],
        out_shape=[
            jax.ShapeDtypeStruct(d.shape, BF16),
            jax.ShapeDtypeStruct((owners, nb, 128), BF16),
            jax.ShapeDtypeStruct((wdim, width), BF16 if later else F32),
        ],
        scratch_shapes=[pltpu.VMEM((wdim, width), F32)],
        input_output_aliases={4: 0, 5: 1} if later else {},
        compiler_params=pltpu.CompilerParams(vmem_limit_bytes=40 * MIB),
        cost_estimate=pl.CostEstimate(
            flops=4 * owners * part * wdim * width,
            bytes_accessed=owners * part * 2 * 1024,
            transcendentals=0,
        ),
        name="owner_backward",
    )(gu, gu, d, wd, *before)


def owner_split_body(*refs):
    *gx_refs, gat_ref, gbt_ref = refs
    narrow = jnp.concatenate([r[...] for r in gx_refs], axis=1).reshape(-1, 128).T
    gbt_ref[...] = narrow[0:64]
    gat_ref[...] = narrow[64:96]


def owner_split(gus, group=8):
    gus = [pltpu.with_memory_space_constraint(gu, pltpu.HBM) for gu in gus]
    owners, _, full = gus[0].shape
    nb = sum(gu.shape[1] for gu in gus)
    total, rows = owners * nb, group * nb
    return pl.pallas_call(
        owner_split_body,
        grid=(owners // group,),
        in_specs=[
            pl.BlockSpec((group, gu.shape[1], 128), lambda i: (i, 0, full // 128 - 1)) for gu in gus
        ],
        out_specs=[
            pl.BlockSpec((32, rows), lambda i: (0, i)),
            pl.BlockSpec((64, rows), lambda i: (0, i)),
        ],
        out_shape=[
            jax.ShapeDtypeStruct((32, total), BF16),
            jax.ShapeDtypeStruct((64, total), BF16),
        ],
        compiler_params=pltpu.CompilerParams(vmem_limit_bytes=40 * MIB),
        cost_estimate=pl.CostEstimate(flops=0, bytes_accessed=total * 2 * 224, transcendentals=0),
        name="owner_split",
    )(*gus)


def exchange(x):
    return lax.all_to_all(x, PLANE, split_axis=0, concat_axis=0, tiled=True)


def shift(x, axis, k):
    n = lax.axis_size(axis)
    return lax.ppermute(x, axis, [(i, (i + k) % n) for i in range(n)])


def add(*parts):
    total = parts[0].astype(F32)
    for p in parts[1:]:
        total = total + p.astype(F32)
    return total


def turn_features(w, y):
    blocks = w.reshape(w.shape[0], 4, 128)
    order = lax.rem(y - jnp.arange(4) + 4, 4)
    return jnp.take(blocks, order, axis=1).reshape(w.shape)


def cross_shift(x, k, swap):
    moves = []
    for z in range(4):
        for xx in range(4):
            for c in range(2):
                along_x = (c == 0) != swap
                to = (z, (xx + k) % 4) if along_x else ((z + k) % 4, xx)
                moves.append((z * 8 + xx * 2 + c, to[0] * 8 + to[1] * 2 + c))
    return lax.ppermute(x, PLANE, moves)


def gather_plane(part):
    part = jnp.concatenate([part] + [cross_shift(part, k, False) for k in (1, 2, 3)])
    pieces = [part] + [cross_shift(part, k, True) for k in (1, 2, 3)]
    first = lax.axis_index("c") == 0
    pieces = jnp.where(first, jnp.stack(pieces), jnp.stack(pieces, axis=1))
    return pieces.reshape((16,) + part.shape[1:])


def scatter_outer(part):
    part = part.reshape((4, 4) + part.shape[1:])
    part = jnp.where(lax.axis_index("c") == 0, part, part.swapaxes(0, 1))
    return [part[0]] + [cross_shift(part[k], -k, True) for k in (1, 2, 3)]


def scatter_inner(part):
    return [part[0]] + [cross_shift(part[k], -k, False) for k in (1, 2, 3)]


def gather_quarters(part):
    below, above = shift(part, "y", 1), shift(part, "y", -1)
    far = jnp.concatenate([shift(below[:8], "y", 1), shift(above[8:], "y", -1)])
    own = (part, below, far, above)
    return own + tuple(shift(p, "c", 1) for p in own)


def scatter_far(own, other):
    s = add(own[2], shift(other[2], "c", 1)).astype(BF16)
    from_above, from_below = shift(s[:8], "y", -1), shift(s[8:], "y", 1)
    s = [add(own[r], shift(other[r], "c", 1)) for r in (0, 1, 3)]
    down = jnp.concatenate([add(s[1][:8], from_above), s[1][8:]]).astype(BF16)
    up = jnp.concatenate([s[2][:8], add(s[2][8:], from_below)]).astype(BF16)
    return s[0], down, up


def scatter_near(own, down, up):
    return add(own, shift(down, "y", -1), shift(up, "y", 1)).astype(BF16)


def on_device(
    pooled_a, pooled_b, pooled_c, pooled_d, proj_a, proj_b, proj_c, proj_d,
    slot_table, norm_gain, grad_gram,
):
    total = pooled_a.shape[0]
    nb = grad_gram.shape[0]
    owners = total // nb
    y = lax.axis_index("y")
    at = jnp.stack([lax.axis_index("z"), lax.axis_index("x"), lax.axis_index("c")]).astype(jnp.int32)
    wd = turn_features(proj_d[0], y)
    gain = turn_features(norm_gain[None], y)
    d = pooled_d[:, 0]
    part = jnp.concatenate([proj_c[0], proj_b[0], proj_a[0]], axis=0)
    part = gather_plane(lax.dynamic_slice_in_dim(part, y * 128, 128, axis=1)[None])
    us = owner_forward(
        pooled_a.transpose(1, 2, 0)[0], pooled_b.transpose(1, 2, 0)[0], pooled_c[:, 0], d, wd, nb
    )
    u0, u1 = us
    start = u0.shape[1]
    u0, part = lax.optimization_barrier((u0, part))
    ws = gather_quarters(part)
    u0 = exchange(u0)
    u1, u0, ws = lax.optimization_barrier((u1, u0, ws))
    u1 = exchange(u1)
    gu0, *gws = middle(0, at, slot_table, gain, u0, ws, grad_gram, [])
    gu0 = exchange(gu0)
    gu1, *gws = middle(start, at, slot_table, gain, u1, ws, grad_gram, gws)
    own, down, up = scatter_far(gws[:4], gws[4:])
    gu1, down, up = lax.optimization_barrier((gu1, down, up))
    gu1 = exchange(gu1)
    d = d.reshape(owners, nb, -1)
    gd, gc, gwd = owner_backward(0, gu0, d, wd)
    part = scatter_near(own, down, up)
    gd, gc, gwd, part = lax.optimization_barrier((gd, gc, gwd, part))
    gd, gc, gwd = owner_backward(start, gu1, d, wd, (gd, gc, gwd))
    gd, gc = gd.reshape(total, -1), gc.reshape(total, -1)
    q = [gwd[:, r * 128 : (r + 1) * 128] for r in range(4)]
    q = [q[0]] + [shift(q[r], "y", -r) for r in (1, 2, 3)]
    pieces, _ = lax.optimization_barrier((scatter_outer(part), gwd))
    pieces = scatter_inner(add(*pieces).astype(BF16))
    gat, gbt = owner_split((gu0, gu1))
    pieces, q, gat, gbt = lax.optimization_barrier((pieces, q, gat, gbt))
    scale = 1.0 / np.sqrt(total * lax.axis_size("y")).astype(np.float32)
    gw = lambda start, stop: add(*[p[None, start:stop] for p in pieces]) * scale
    gwd = add(*q) * scale
    return (
        gat.T[:, None],
        gbt.T[:, None],
        gc[:, None],
        gd[:, None],
        gw(192, 224),
        gw(128, 192),
        gw(0, 128),
        gwd[None],
    )


def solution(mesh):
    fine = Mesh(np.array(mesh.devices).reshape(4, 4, 4, 2), ("y", "z", "x", "c"))
    pooled = P("y", PLANE, None)
    weight = P(PLANE, None, None)
    in_specs = (pooled,) * 4 + (weight,) * 4 + (P(), P(), P(("y",) + PLANE, None, None))
    out_specs = (pooled,) * 4 + (P(PLANE, None, "y"),) * 4
    return jax.shard_map(
        on_device, mesh=fine, in_specs=in_specs, out_specs=out_specs, check_vma=False
    )
```
